512 devices in a mesh: row: 32 (over y_lo, z, core), col: 16 (over y_hi, x).
Axes of the slice: x: 4, y: 8 (y_hi: 4, y_lo: 2; y = y_hi * 2 + y_lo), z: 8, core: 2. Of those that a mesh axis runs over, the one named last changes fastest.
Arguments:
- normed: bfloat16 [768, 8192], P('col', 'row'), may hold values from -6 to 6
- gate_w: bfloat16 [8192, 14336], P('row', 'col'), may hold values from -0.0625 to 0.0625
- up_w: bfloat16 [8192, 14336], P('row', 'col'), may hold values from -0.0625 to 0.0625
- down_w: bfloat16 [14336, 8192], P('col', 'row'), may hold values from -0.046875 to 0.046875
- gate_pre: bfloat16 [768, 14336], P('row', 'col'), may hold values from -8 to 8
- up_pre: bfloat16 [768, 14336], P('row', 'col'), may hold values from -6 to 6
- block_out: bfloat16 [768, 8192], P('col', 'row'), may hold values from -6 to 6
- value_w: float32 [8192], P('row'), may hold values from -2 to 2
- q_target: float32 [768], P('col'), may hold values from -10 to 10
- grad_out: bfloat16 [768, 8192], P('col', 'row'), may hold values from -6 to 6
Outputs:
- grad_normed: bfloat16 [768, 8192], P('col', 'row')
- grad_gate: bfloat16 [8192, 14336], P('row', 'col')
- grad_up: bfloat16 [8192, 14336], P('row', 'col')
- grad_down: bfloat16 [14336, 8192], P('col', 'row')
The draws below stay inside these ranges and needn't reach their ends.
All inputs are finite; a program needn't handle non-finite values.
Results may differ from the reference program's by a relative error of at most 0.0058.
Values may be sent and summed in bfloat16 or wider, within the bound.
A program may use at most 64 MiB of HBM per device.

```python
import math
import jax
import jax.numpy as jnp
from jax import lax

D = 8192
FF = 14336
TOKENS = 768


def draw_value_w(key, part):
    key = jax.random.fold_in(key, 11)
    position = jnp.arange(D, dtype=jnp.float32) / D
    base = jnp.clip(jax.random.normal(key, (D,), jnp.float32), -4.0, 4.0)
    rising = jnp.exp(position * math.log(3.0))
    return (base * rising * (1.0 / math.sqrt(D))).astype(jnp.float32)


def levels(stream_key, extent, cuts, low, high):
    gain, own = 1.0, jax.random.fold_in(stream_key, 6)
    for axis_at, shards_of in cuts:
        draws = jnp.exp(jax.random.uniform(jax.random.fold_in(own, axis_at), (shards_of,), jnp.float32, low / len(cuts), high / len(cuts)))
        gain = gain * jnp.repeat(draws, extent[axis_at] // shards_of).reshape([-1 if axis == axis_at else 1 for axis in range(len(extent))])
    return gain


def gaussian(stream_key, extent, spread, limit, pieces=(), held_as=jnp.bfloat16):
    entries = spread * jax.random.normal(stream_key, extent, jnp.float32)
    if pieces:
        entries = entries * levels(stream_key, extent, pieces, -0.22, 0.18)
    return jnp.clip(entries, -limit, limit).astype(held_as)


def setup_inputs(seed: int = 0) -> dict:
    key_of = jax.random.split(jax.random.key(seed), 11)
    return {
        "normed": gaussian(key_of[0], (TOKENS, D), 1.0, 6.0, ((0, 16), (1, 32))),
        "gate_w": gaussian(key_of[1], (D, FF), D ** -0.5, 0.0625, ((0, 32), (1, 16))),
        "up_w": gaussian(key_of[2], (D, FF), D ** -0.5, 0.0625, ((0, 32), (1, 16))),
        "down_w": gaussian(key_of[3], (FF, D), FF ** -0.5, 0.046875, ((0, 16), (1, 32))),
        "gate_pre": gaussian(key_of[4], (TOKENS, FF), 2.0, 8.0, ((0, 32), (1, 16))),
        "up_pre": gaussian(key_of[5], (TOKENS, FF), 1.0, 6.0, ((0, 32), (1, 16))),
        "block_out": gaussian(key_of[6], (TOKENS, D), 1.0, 6.0, ((0, 16), (1, 32))),
        "value_w": draw_value_w(jax.random.fold_in(key_of[10], 71), 0),
        "q_target": gaussian(key_of[8], (TOKENS,), 2.0, 10.0, ((0, 16),), jnp.float32),
        "grad_out": gaussian(key_of[9], (TOKENS, D), 1.0, 6.0, ((0, 16), (1, 32))),
    }


expectile = 0.7
value_scale = 8.0

def output_grad(value_w, q_target, grad_out, value_est):
    margin = q_target - value_est
    weighting = jnp.where(margin > 0, expectile, 1.0 - expectile)
    value_grad = -2.0 * value_scale * weighting * margin
    return (grad_out.astype(jnp.float32) + value_grad[:, None] * value_w[None, :]).astype(jnp.bfloat16)

def swiglu_back(hidden_grad, gate_pre, up_pre):
    gate_val = gate_pre.astype(jnp.float32)
    up_val = up_pre.astype(jnp.float32)
    sigmoid_val = jax.nn.sigmoid(gate_val)
    silu_val = gate_val * sigmoid_val
    act_out = (silu_val * up_val).astype(jnp.bfloat16)
    gate_back = (hidden_grad * up_val * sigmoid_val * (1.0 + gate_val * (1.0 - sigmoid_val))).astype(jnp.bfloat16)
    up_back = (hidden_grad * silu_val).astype(jnp.bfloat16)
    return (gate_back, up_back, act_out)

def reference(normed, gate_w, up_w, down_w, gate_pre, up_pre, block_out, value_w, q_target, grad_out):
    contract_last = (((1,), (1,)), ((), ()))
    contract_first = (((0,), (0,)), ((), ()))
    value_est = jnp.dot(block_out.astype(jnp.float32), value_w, precision=lax.Precision.HIGHEST)
    out_grad = output_grad(value_w, q_target, grad_out, value_est)
    hidden_grad = lax.dot_general(out_grad, down_w, contract_last, preferred_element_type=jnp.float32)
    gate_back, up_back, act_out = swiglu_back(hidden_grad, gate_pre, up_pre)
    grad_normed = lax.dot_general(gate_back, gate_w, contract_last, preferred_element_type=jnp.float32)
    grad_normed = grad_normed + lax.dot_general(up_back, up_w, contract_last, preferred_element_type=jnp.float32)
    grad_gate = lax.dot_general(normed, gate_back, contract_first, preferred_element_type=jnp.float32)
    grad_up = lax.dot_general(normed, up_back, contract_first, preferred_element_type=jnp.float32)
    grad_down = lax.dot_general(act_out, out_grad, contract_first, preferred_element_type=jnp.float32)
    return (grad_normed.astype(jnp.bfloat16), grad_gate.astype(jnp.bfloat16), grad_up.astype(jnp.bfloat16), grad_down.astype(jnp.bfloat16))
```

```python
import jax
import jax.numpy as jnp
from jax import lax
from jax.experimental import pallas as pl
from jax.experimental.pallas import tpu as pltpu
from jax.sharding import PartitionSpec as P

expectile = 0.7
value_scale = 8.0

F32 = jnp.float32
BF16 = jnp.bfloat16
CUT = 512
N_COPIES = 256

NT = (((1,), (1,)), ((), ()))
TN = (((0,), (0,)), ((), ()))


def dot_nt(a, b):
    return lax.dot_general(a, b, NT, preferred_element_type=F32)


def dot_tn(a, b):
    return lax.dot_general(a, b, TN, preferred_element_type=F32)


def kernel(
    normed_h, gate_w_h, up_w_h, down_w_h, gate_pre, up_pre, block_out, value_w, q_target, grad_out_h,
    o_normed, o_gate, o_up, o_down,
    GO, NO, GU, gw, uw, dw,
    PK, SIN, PO, SB, RA1, RA2, RB1, RB2, RF, YS, YR, HA,
    SIL, GF, ACT, GB, UB, OG,
    CS, RX, TS, RY,
    M0, MS, M1, MY, M2, MZ, VG, U,
    local, ss, rs,
):
    row, col = lax.axis_index("row"), lax.axis_index("col")
    k, z, yl = row % 2, (row // 2) % 8, row // 16
    x, yh = col % 4, col // 4

    def dev(k_=k, z_=z, yl_=yl, x_=x, yh_=yh):
        return ((yl_ * 8 + z_) * 2 + k_, yh_ * 4 + x_)

    def zd(d):
        return (z + d + 8) % 8

    def xd(d):
        return (x + d + 4) % 4

    def yd(d):
        return (yh + d + 4) % 4

    sib = dev(k_=1 - k)
    ylp = dev(yl_=1 - yl)
    zdev = {d: dev(z_=zd(d)) for d in (1, -1, 2, -2, 3, -3, 4)}
    xdev = {d: dev(x_=xd(d)) for d in (1, 2, 3)}
    ydev = {d: dev(yh_=yd(d)) for d in (1, 2, 3)}

    started = []

    def send(src, dst, to):
        i = len(started)
        cp = pltpu.make_async_remote_copy(
            src, dst, ss.at[i], rs.at[i], device_id=to, device_id_type=pl.DeviceIdType.MESH
        )
        cp.start()
        started.append(cp)
        return cp

    loads = []

    def load(src, dst):
        cp = pltpu.make_async_copy(src, dst, local.at[len(loads)])
        cp.start()
        loads.append(cp)
        return cp

    l_go = load(grad_out_h, GO.at[col])
    l_dw = load(down_w_h, dw)
    l_no = load(normed_h, NO.at[col])
    l_gw = load(gate_w_h, gw)
    l_uw = load(up_w_h, uw)

    barrier = pltpu.get_barrier_semaphore()
    partners = [sib, ylp, *zdev.values(), *xdev.values(), *ydev.values()]
    for p in partners:
        pl.semaphore_signal(barrier, inc=1, device_id=p, device_id_type=pl.DeviceIdType.MESH)

    GU[row] = jnp.concatenate([gate_pre[...].astype(F32), up_pre[...].astype(F32)], axis=0).astype(BF16)
    l_go.wait()
    pl.semaphore_wait(barrier, len(partners))

    def gather_y(buf):
        cy = {d: send(buf.at[col], buf.at[col], ydev[d]) for d in (1, 3, 2)}
        cx = {(0, d): send(buf.at[col], buf.at[col], xdev[d]) for d in (1, 3, 2)}
        return cy, cx

    def gather_x(buf, cy, cx):
        for dy in (1, 3, 2):
            cy[dy].wait_recv()
            at = yd(-dy) * 4 + x
            for d in (1, 3, 2):
                cx[(dy, d)] = send(buf.at[at], buf.at[at], xdev[d])

    def gather_end(cx):
        for cp in cx.values():
            cp.wait_recv()

    def z_start(buf, at):
        a = at(0)
        return {d: send(buf.at[a], buf.at[a], zdev[d]) for d in (2, -2, 1, -1)}

    def z_relay(buf, at, st):
        out = {}
        st[2].wait_recv()
        a = at(-2)
        out[3] = send(buf.at[a], buf.at[a], zdev[1])
        out["a"] = send(buf.at[a, :, :CUT], buf.at[a, :, :CUT], zdev[2])
        st[-2].wait_recv()
        a = at(2)
        out[-3] = send(buf.at[a], buf.at[a], zdev[-1])
        out["b"] = send(buf.at[a, :, CUT:], buf.at[a, :, CUT:], zdev[-2])
        return out

    cy, cx = gather_y(GO)

    def gu_at(kk, yy):
        return lambda d: (yy * 8 + zd(d)) * 2 + kk

    mine = gu_at(k, yl)
    st = z_start(GU, mine)
    gu_y, gu_s, gu_s2 = {}, {}, {}

    def gu_forward(d):
        a = mine(d)
        gu_y[d] = send(GU.at[a], GU.at[a], ylp)
        gu_s[d] = send(GU.at[a], GU.at[a], sib)

    def gu_forward2(d):
        gu_y[d].wait_recv()
        a = gu_at(k, 1 - yl)(d)
        gu_s2[d] = send(GU.at[a], GU.at[a], sib)

    gu_forward(0)

    l_dw.wait()
    vw = value_w[...]
    hi = vw.astype(BF16).astype(F32)
    mid = (vw - hi).astype(BF16).astype(F32)
    lo = vw - hi - mid
    terms = jnp.concatenate([hi, mid, lo, jnp.zeros((5, 256), F32)], axis=0).astype(BF16)
    u_part = jnp.sum(dot_nt(terms, dw[...]), axis=0, keepdims=True)
    v_part = jnp.sum(dot_nt(terms, block_out[...]), axis=0, keepdims=True)
    M0[...] = jnp.zeros((8, 128), F32)
    for i in range(7):
        M0[i : i + 1, :] = u_part[:, 128 * i : 128 * (i + 1)]
    M0[7:8, 0:48] = v_part
    m_s = send(M0, MS, sib)

    gather_x(GO, cy, cx)

    m_s.wait_recv()
    M1[...] = M0[...] + MS[...]
    m_y = send(M1, MY, ylp)

    relay = z_relay(GU, mine, st)

    m_y.wait_recv()
    M2[...] = M1[...] + MY[...]
    m_z = [send(M2, MZ.at[i], zdev[d]) for i, d in enumerate((4, 3, -3, 2, -2, 1, -1))]

    gu_forward(-2)
    gu_forward(2)
    st[1].wait_recv()
    gu_forward(-1)
    st[-1].wait_recv()
    gu_forward(1)

    gather_end(cx)

    order = (3, -3, 4, 2, -2, 1, -1, 0)
    slot = {d: i for i, d in enumerate(order)}
    sib_copy = {}
    for d0, d1 in ((3, -3), (4, 2), (-2, 1), (-1, 0)):
        a = jnp.concatenate([GO[(1 - k) * 8 + zd(d0)], GO[(1 - k) * 8 + zd(d1)]], axis=0)
        p = dot_nt(a, dw[...]).astype(BF16)
        PK[slot[d0]] = p[:48]
        PK[slot[d1]] = p[48:]
        sib_copy[d0] = send(PK.at[slot[d0]], SIN.at[slot[d0]], sib)
        sib_copy[d1] = send(PK.at[slot[d1]], SIN.at[slot[d1]], sib)
    for d0, d1 in ((3, -3), (4, 2), (-2, 1), (-1, 0)):
        a = jnp.concatenate([GO[k * 8 + zd(d0)], GO[k * 8 + zd(d1)]], axis=0)
        p = dot_nt(a, dw[...])
        PO[slot[d0]] = p[:48]
        PO[slot[d1]] = p[48:]

    def pair_sum(d):
        sib_copy[d].wait_recv()
        return PO[slot[d]] + SIN[slot[d]].astype(F32)

    SB[slot[3]] = pair_sum(3).astype(BF16)
    r_a1 = send(SB.at[slot[3]], RA1, zdev[1])
    SB[slot[-3]] = pair_sum(-3).astype(BF16)
    r_b1 = send(SB.at[slot[-3]], RB1, zdev[-1])
    SB[slot[4]] = pair_sum(4).astype(BF16)
    r_a2 = send(SB.at[slot[4], :, :CUT], RA2, zdev[2])
    r_b2 = send(SB.at[slot[4], :, CUT:], RB2, zdev[-2])
    SB[slot[1]] = pair_sum(1).astype(BF16)
    f_1 = send(SB.at[slot[1]], RF.at[0], zdev[1])
    SB[slot[-1]] = pair_sum(-1).astype(BF16)
    f_m1 = send(SB.at[slot[-1]], RF.at[1], zdev[-1])
    s2 = pair_sum(2)
    r_a1.wait_recv()
    r_a2.wait_recv()
    SB[slot[2], :, :CUT] = (s2[:, :CUT] + RA1[:, :CUT].astype(F32) + RA2[...].astype(F32)).astype(BF16)
    SB[slot[2], :, CUT:] = (s2[:, CUT:] + RA1[:, CUT:].astype(F32)).astype(BF16)
    f_2 = send(SB.at[slot[2]], RF.at[2], zdev[2])
    sm2 = pair_sum(-2)
    r_b1.wait_recv()
    r_b2.wait_recv()
    SB[slot[-2], :, :CUT] = (sm2[:, :CUT] + RB1[:, :CUT].astype(F32)).astype(BF16)
    SB[slot[-2], :, CUT:] = (sm2[:, CUT:] + RB1[:, CUT:].astype(F32) + RB2[...].astype(F32)).astype(BF16)
    f_m2 = send(SB.at[slot[-2]], RF.at[3], zdev[-2])

    l_no.wait()
    ny, nx = gather_y(NO)
    relay[3].wait_recv()
    gu_forward(-3)
    relay[-3].wait_recv()
    gu_forward(3)
    relay["a"].wait_recv()
    relay["b"].wait_recv()
    gu_forward(4)
    for cp in m_z:
        cp.wait_recv()
    total = M2[...]
    for i in range(7):
        total = total + MZ[i]
    for i in range(7):
        U[:, 128 * i : 128 * (i + 1)] = total[i : i + 1, :]
    margin = q_target[...] - total[7:8, 0:48]
    weighting = jnp.where(margin > 0, expectile, 1.0 - expectile)
    VG[col] = jnp.zeros((8, 128), F32)
    VG[col, 0:1, 0:48] = -2.0 * value_scale * weighting * margin
    vy, vx = gather_y(VG)
    gather_x(NO, ny, nx)
    for d in (0, -2, 2, -1, 1, -3, 3, 4):
        gu_forward2(d)
    gather_x(VG, vy, vx)

    for cp in (f_1, f_m1, f_2, f_m2):
        cp.wait_recv()
    s0 = pair_sum(0)
    for i in range(4):
        s0 = s0 + RF[i].astype(F32)
    YS[...] = s0.astype(BF16)
    y_c = send(YS, YR, ylp)

    for d in (0, -2, 2, -1, 1, -3, 3, 4):
        gu_s[d].wait_recv()
        gu_s2[d].wait_recv()

    def factors(j, carry):
        a = GU[2 * j].astype(F32)
        b = GU[2 * j + 1].astype(F32)
        gate = jnp.concatenate([a[:24], b[:24]], axis=0)
        up = jnp.concatenate([a[24:], b[24:]], axis=0)
        s = jax.nn.sigmoid(gate)
        silu = gate * s
        SIL[j] = silu
        ACT[j] = (silu * up).astype(BF16)
        GF[j] = up * s * (1.0 + gate * (1.0 - s))
        return carry

    lax.fori_loop(0, 8, factors, 0)

    y_c.wait_recv()
    me = k * 8 + z
    HA[me] = (YS[...].astype(F32) + YR[...].astype(F32)).astype(BF16)

    def h_at(d):
        return k * 8 + zd(d)

    hst = z_start(HA, h_at)
    h_s = {}

    def h_forward(d):
        h_s[d] = send(HA.at[h_at(d)], HA.at[h_at(d)], sib)

    h_forward(0)
    lax.fori_loop(8, 12, factors, 0)
    hrel = z_relay(HA, h_at, hst)
    h_forward(-2)
    h_forward(2)
    hst[1].wait_recv()
    h_forward(-1)
    hst[-1].wait_recv()
    h_forward(1)
    lax.fori_loop(12, 16, factors, 0)

    gather_end(vx)

    def value_col(j):
        return VG[j].T[:48, 0:1]

    def out_grad(j, carry):
        OG[j] = (GO[j].astype(F32) + value_col(j) * vw).astype(BF16)
        return carry

    lax.fori_loop(0, 16, out_grad, 0)
    o_down[...] = dot_tn(ACT[...].reshape(768, 896), OG[...].reshape(768, 256)).astype(BF16)

    hrel[3].wait_recv()
    h_forward(-3)
    hrel[-3].wait_recv()
    h_forward(3)
    hrel["a"].wait_recv()
    hrel["b"].wait_recv()
    h_forward(4)
    for cp in h_s.values():
        cp.wait_recv()

    l_gw.wait()
    l_uw.wait()

    def back(j):
        h = HA[j].astype(F32) + value_col(j) * U[...]
        GB[j] = (h * GF[j]).astype(BF16)
        UB[j] = (h * SIL[j]).astype(BF16)

    own = None
    x_c = {}
    for d in (2, 1, 3, 0):
        for q in range(4):
            back(q * 4 + xd(d))
        g = jnp.concatenate([GB[q * 4 + xd(d)] for q in range(4)], axis=0)
        u = jnp.concatenate([UB[q * 4 + xd(d)] for q in range(4)], axis=0)
        part = (dot_nt(g, gw[...]) + dot_nt(u, uw[...])).reshape(4, 48, 256)
        if d:
            CS[d - 1] = part.astype(BF16)
            x_c[d] = send(CS.at[d - 1], RX.at[d - 1], xdev[d])
        else:
            own = part
    gather_end(nx)
    o_gate[...] = dot_tn(NO[...].reshape(768, 256), GB[...].reshape(768, 896)).astype(BF16)
    for d in (1, 2, 3):
        x_c[d].wait_recv()
        own = own + RX[d - 1].astype(F32)
    TS[...] = own
    y_s = {}
    for d in (2, 1, 3):
        CS[3, d] = TS[yd(d)].astype(BF16)
        y_s[d] = send(CS.at[3, d], RY.at[d - 1], ydev[d])
    o_up[...] = dot_tn(NO[...].reshape(768, 256), UB[...].reshape(768, 896)).astype(BF16)
    out = TS[yh]
    for d in (1, 2, 3):
        y_s[d].wait_recv()
        out = out + RY[d - 1].astype(F32)
    o_normed[...] = out.astype(BF16)

    for cp in started:
        cp.wait_send()


def per_device(normed, gate_w, up_w, down_w, gate_pre, up_pre, block_out, value_w, q_target, grad_out):
    hbm = pl.BlockSpec(memory_space=pl.ANY)
    vmem = pl.BlockSpec(memory_space=pltpu.VMEM)
    scratch = [
        pltpu.VMEM((16, 48, 256), BF16),
        pltpu.VMEM((16, 48, 256), BF16),
        pltpu.VMEM((32, 48, 896), BF16),
        pltpu.VMEM((256, 896), BF16),
        pltpu.VMEM((256, 896), BF16),
        pltpu.VMEM((896, 256), BF16),
        pltpu.VMEM((8, 48, 896), BF16),
        pltpu.VMEM((8, 48, 896), BF16),
        pltpu.VMEM((8, 48, 896), F32),
        pltpu.VMEM((8, 48, 896), BF16),
        pltpu.VMEM((48, 896), BF16),
        pltpu.VMEM((48, CUT), BF16),
        pltpu.VMEM((48, 896), BF16),
        pltpu.VMEM((48, 896 - CUT), BF16),
        pltpu.VMEM((4, 48, 896), BF16),
        pltpu.VMEM((48, 896), BF16),
        pltpu.VMEM((48, 896), BF16),
        pltpu.VMEM((16, 48, 896), BF16),
        pltpu.VMEM((16, 48, 896), F32),
        pltpu.VMEM((16, 48, 896), F32),
        pltpu.VMEM((16, 48, 896), BF16),
        pltpu.VMEM((16, 48, 896), BF16),
        pltpu.VMEM((16, 48, 896), BF16),
        pltpu.VMEM((16, 48, 256), BF16),
        pltpu.VMEM((4, 4, 48, 256), BF16),
        pltpu.VMEM((3, 4, 48, 256), BF16),
        pltpu.VMEM((4, 48, 256), F32),
        pltpu.VMEM((3, 48, 256), BF16),
        pltpu.VMEM((8, 128), F32),
        pltpu.VMEM((8, 128), F32),
        pltpu.VMEM((8, 128), F32),
        pltpu.VMEM((8, 128), F32),
        pltpu.VMEM((8, 128), F32),
        pltpu.VMEM((7, 8, 128), F32),
        pltpu.VMEM((16, 8, 128), F32),
        pltpu.VMEM((1, 896), F32),
        pltpu.SemaphoreType.DMA((5,)),
        pltpu.SemaphoreType.DMA((N_COPIES,)),
        pltpu.SemaphoreType.DMA((N_COPIES,)),
    ]
    return pl.pallas_call(
        kernel,
        out_shape=(
            jax.ShapeDtypeStruct((48, 256), BF16),
            jax.ShapeDtypeStruct((256, 896), BF16),
            jax.ShapeDtypeStruct((256, 896), BF16),
            jax.ShapeDtypeStruct((896, 256), BF16),
        ),
        in_specs=[hbm, hbm, hbm, hbm, vmem, vmem, vmem, vmem, vmem, hbm],
        out_specs=(vmem, vmem, vmem, vmem),
        scratch_shapes=scratch,
        compiler_params=pltpu.CompilerParams(
            collective_id=0, has_side_effects=True, vmem_limit_bytes=48 * 2**20
        ),
    )(
        normed, gate_w, up_w, down_w, gate_pre, up_pre, block_out,
        value_w.reshape(1, 256), q_target.reshape(1, 48), grad_out,
    )


def solution(mesh):
    return jax.shard_map(
        per_device,
        mesh=mesh,
        in_specs=(
            P("col", "row"),
            P("row", "col"),
            P("row", "col"),
            P("col", "row"),
            P("row", "col"),
            P("row", "col"),
            P("col", "row"),
            P("row"),
            P("col"),
            P("col", "row"),
        ),
        out_specs=(P("col", "row"), P("row", "col"), P("row", "col"), P("col", "row")),
        check_vma=False,
    )
```

```python
import jax
import jax.numpy as jnp
from jax import lax
from jax.experimental import pallas as pl
from jax.experimental.pallas import tpu as pltpu
from jax.sharding import PartitionSpec as P

expectile = 0.7
value_scale = 8.0

F32 = jnp.float32
BF16 = jnp.bfloat16
MESH = pl.DeviceIdType.MESH

PARTS = ((0, 256, 512), (512, 640, 896))
CUT = 512
N_SEND = 16
N_RECV = 56
N_LOCAL = 9
DIRECT = False

NT = (((1,), (1,)), ((), ()))
TN = (((0,), (0,)), ((), ()))

def dot_nt(a, b):
    return lax.dot_general(a, b, NT, preferred_element_type=F32)

def dot_tn(a, b):
    return lax.dot_general(a, b, TN, preferred_element_type=F32)

def dot(a, b):
    return jnp.dot(a, b, preferred_element_type=F32)

def kernel(
    normed_h, gate_w_h, up_w_h, down_w_h, gate_pre, up_pre, block_out, value_w, q_target, grad_out_h,
    o_normed_h, o_gate_h, o_up_h, o_down_h,
    GO, NO, GU, gw, uw, dw, GWT, UWT, NOT,
    PK, SIN, PO, SB, RA1, RA2, RB1, RB2, RF, OWNH, YS, YR, HA,
    SIL, GF, ACT, GB, UB, OG,
    CS, RIN, OWN, o_normed, o_gate, o_up, o_down,
    M0, MS, M1, MY, M2, MZ, VG, VC, U,
    local, ss, rs,
):
    row, col = lax.axis_index("row"), lax.axis_index("col")
    k, z, yl = row % 2, (row // 2) % 8, row // 16
    x, yh = col % 4, col // 4

    def dev(k_=k, z_=z, yl_=yl, x_=x, yh_=yh):
        return ((yl_ * 8 + z_) * 2 + k_, yh_ * 4 + x_)

    def zd(d):
        return (z + d + 8) % 8

    def xd(d):
        return (x + d + 4) % 4

    def yd(d):
        return (yh + d + 4) % 4

    sib = dev(k_=1 - k)
    ylp = dev(yl_=1 - yl)
    zdev = {d: dev(z_=zd(d)) for d in (1, -1, 2, -2, 3, -3, 4)}
    xdev = {d: dev(x_=xd(d)) for d in (1, 2, 3)}
    ydev = {d: dev(yh_=yd(d)) for d in (1, 2, 3)}

    ids = {"send": {}, "recv": {}}
    started, arrived, loads = [], set(), []

    def sem(side, name):
        known = ids[side]
        if name not in known:
            known[name] = len(known)
            assert len(known) <= (N_SEND if side == "send" else N_RECV)
        return (ss if side == "send" else rs).at[known[name]]

    def remote(src, dst, group, name, to):
        return pltpu.make_async_remote_copy(
            src, dst, sem("send", group), sem("recv", name), device_id=to, device_id_type=MESH
        )

    def send(src, dst, group, name, to):
        cp = remote(src, dst, group, name, to)
        cp.start()
        started.append((cp, name))

    def came(name, ref):
        remote(ref, ref, "none", name, sib).wait_recv()
        arrived.add(name)

    def left(group, ref):
        remote(ref, ref, group, "none", sib).wait_send()

    def load(src, dst):
        cp = pltpu.make_async_copy(src, dst, local.at[len(loads)])
        cp.start()
        loads.append(cp)
        return cp

    def finish():
        for cp in loads:
            if all(cp is not w for w in waited):
                cp.wait()
        for cp, name in started:
            cp.wait_send()
            if name not in arrived:
                cp.wait_recv()

    waited = []

    def ready(*cps):
        for cp in cps:
            cp.wait()
            waited.append(cp)

    l_go = load(grad_out_h, GO.at[col])
    l_dw = load(down_w_h, dw)
    l_no = load(normed_h, NO.at[col])
    l_gw = load(gate_w_h, gw)
    l_uw = load(up_w_h, uw)

    barrier = pltpu.get_barrier_semaphore()
    partners = [sib, ylp, *zdev.values()] + [(row, (col + i) % 16) for i in range(1, 16)]
    for p in partners:
        pl.semaphore_signal(barrier, inc=1, device_id=p, device_id_type=MESH)

    GU[yl, z, k] = jnp.concatenate([gate_pre[...].astype(F32), up_pre[...].astype(F32)], axis=0).astype(BF16)
    ready(l_go)
    pl.semaphore_wait(barrier, len(partners))

    def gather_direct(buf, group, name):
        for i in (10, 6, 14, 2, 9, 11, 5, 7, 13, 15, 1, 3, 8, 4, 12):
            send(buf.at[col], buf.at[col], group, name, (row, (col + i) % 16))

    def gather_y(buf, group, name):
        for d in (2, 1, 3):
            send(buf.at[col], buf.at[col], group, name + str(d), ydev[d])
        for d in (2, 1, 3):
            send(buf.at[col], buf.at[col], group, name, xdev[d])

    def gather_x(buf, group, name):
        for dy in (1, 3, 2):
            at = yd(-dy) * 4 + x
            came(name + str(dy), buf.at[at])
            for d in (2, 1, 3):
                send(buf.at[at], buf.at[at], group, name, xdev[d])

    if DIRECT:
        gather_direct(GO, "go", "go")
    else:
        gather_y(GO, "go", "go")

    def gu(d):
        return GU.at[yl, zd(d), k]

    def gu_y(d):
        send(gu(d), gu(d), "guy", "guy", ylp)

    for d, name in ((2, "gu+2"), (-2, "gu-2"), (1, "gu1"), (-1, "gu1")):
        send(gu(0), gu(0), "guz", name, zdev[d])
    if not DIRECT:
        gu_y(0)

    ready(l_dw)
    vw = value_w[...]
    hi = vw.astype(BF16).astype(F32)
    mid = (vw - hi).astype(BF16).astype(F32)
    lo = vw - hi - mid
    terms = jnp.concatenate([hi, mid, lo, jnp.zeros((5, 256), F32)], axis=0).astype(BF16)
    u_part = jnp.sum(dot_nt(terms, dw[...]), axis=0, keepdims=True)
    v_part = jnp.sum(dot_nt(terms, block_out[...]), axis=0, keepdims=True)
    M0[...] = jnp.zeros((8, 128), F32)
    for i in range(7):
        M0[i : i + 1, :] = u_part[:, 128 * i : 128 * (i + 1)]
    M0[7:8, 0:48] = v_part
    send(M0, MS, "m0", "m0", sib)

    if not DIRECT:
        gather_x(GO, "go", "go")

    came("m0", MS)
    M1[...] = M0[...] + MS[...]
    send(M1, MY, "m1", "m1", ylp)

    came("gu+2", gu(-2))
    send(gu(-2), gu(-2), "guz", "gu3", zdev[1])
    send(gu(-2).at[:, :CUT], gu(-2).at[:, :CUT], "guz", "gu3", zdev[2])
    came("gu-2", gu(2))
    send(gu(2), gu(2), "guz", "gu3", zdev[-1])
    send(gu(2).at[:, CUT:], gu(2).at[:, CUT:], "guz", "gu3", zdev[-2])

    came("m1", MY)
    M2[...] = M1[...] + MY[...]
    for i, d in enumerate((4, 3, -3, 2, -2, 1, -1)):
        send(M2, MZ.at[i], "m2", "m2", zdev[d])

    if not DIRECT:
        gu_y(-2)
        gu_y(2)
        came("gu1", GU.at[0, 0:2, 0])
        gu_y(-1)
        gu_y(1)

    if DIRECT:
        came("go", GO.at[0:15])
    else:
        came("go", GO.at[0:12])

    order = (3, -3, 4, 2, -2, 1, -1, 0)
    slot = {d: i for i, d in enumerate(order)}
    pairs = ((3, -3), (4, 2), (-2, 1), (-1, 0))
    for h, (lo, _, up) in enumerate(PARTS):
        for i, (d0, d1) in enumerate(pairs):
            a = jnp.concatenate([GO[(1 - k) * 8 + zd(d0)], GO[(1 - k) * 8 + zd(d1)]], axis=0)
            p = dot_nt(a, dw[lo:up]).astype(BF16)
            PK[2 * i, :, lo:up] = p[:48]
            PK[2 * i + 1, :, lo:up] = p[48:]
            at = pl.ds(2 * i, 2)
            send(PK.at[at, :, lo:up], SIN.at[at, :, lo:up], "pk", ("sin", i, h), sib)
        for i, (d0, d1) in enumerate(pairs):
            a = jnp.concatenate([GO[k * 8 + zd(d0)], GO[k * 8 + zd(d1)]], axis=0)
            p = dot_nt(a, dw[lo:up])
            PO[2 * i, :, lo:up] = p[:48]
            PO[2 * i + 1, :, lo:up] = p[48:]

    def pair_sum(d, h):
        lo, _, up = PARTS[h]
        i = slot[d] // 2
        if ("sin", i, h) not in arrived:
            came(("sin", i, h), SIN.at[pl.ds(2 * i, 2), :, lo:up])
        return PO[slot[d], :, lo:up] + SIN[slot[d], :, lo:up].astype(F32)

    def rs_first(h):
        lo, cut, up = PARTS[h]
        for d in (3, -3, 4):
            SB[slot[d], :, lo:up] = pair_sum(d, h).astype(BF16)
            src = SB.at[slot[d]]
            if d == 3:
                send(src.at[:, lo:up], RA1.at[:, lo:up], "rs", ("a1", h), zdev[1])
            elif d == -3:
                send(src.at[:, lo:up], RB1.at[:, lo:up], "rs", ("b1", h), zdev[-1])
            else:
                send(src.at[:, lo:cut], RA2.at[:, lo:cut], "rs", ("a2", h), zdev[2])
                send(src.at[:, cut:up], RB2.at[:, cut:up], "rs", ("b2", h), zdev[-2])

    def rs_near(h):
        lo, cut, up = PARTS[h]
        for i, d in enumerate((1, -1)):
            SB[slot[d], :, lo:up] = pair_sum(d, h).astype(BF16)
            send(SB.at[slot[d], :, lo:up], RF.at[i, :, lo:up], "rs", ("rf", h), zdev[d])

    def rs_second(h):
        lo, cut, up = PARTS[h]
        t = pair_sum(2, h)
        came(("a1", h), RA1.at[:, lo:up])
        came(("a2", h), RA2.at[:, lo:cut])
        t = t + RA1[:, lo:up].astype(F32)
        SB[slot[2], :, lo:cut] = (t[:, : cut - lo] + RA2[:, lo:cut].astype(F32)).astype(BF16)
        SB[slot[2], :, cut:up] = t[:, cut - lo :].astype(BF16)
        send(SB.at[slot[2], :, lo:up], RF.at[2, :, lo:up], "rs", ("rf", h), zdev[2])
        t = pair_sum(-2, h)
        came(("b1", h), RB1.at[:, lo:up])
        came(("b2", h), RB2.at[:, cut:up])
        t = t + RB1[:, lo:up].astype(F32)
        SB[slot[-2], :, lo:cut] = t[:, : cut - lo].astype(BF16)
        SB[slot[-2], :, cut:up] = (t[:, cut - lo :] + RB2[:, cut:up].astype(F32)).astype(BF16)
        send(SB.at[slot[-2], :, lo:up], RF.at[3, :, lo:up], "rs", ("rf", h), zdev[-2])

    rs_first(0)
    rs_first(1)
    rs_near(0)
    rs_second(0)
    rs_near(1)
    rs_second(1)

    if DIRECT:
        for d in (0, -2, 2):
            gu_y(d)
        came("gu1", GU.at[0, 0:2, 0])
        gu_y(-1)
        gu_y(1)
    came("gu3", GU.at[0, 0:3, 0])
    for d in (-3, 3, 4):
        gu_y(d)
    send(GU.at[yl, :, k], GU.at[yl, :, k], "gus", "gus1", sib)
    came("m2", MZ)
    total = M2[...]
    for i in range(7):
        total = total + MZ[i]
    for i in range(7):
        U[:, 128 * i : 128 * (i + 1)] = total[i : i + 1, :]
    margin = q_target[...] - total[7:8, 0:48]
    weighting = jnp.where(margin > 0, expectile, 1.0 - expectile)
    VG[col] = jnp.zeros((8, 128), F32)
    VG[col, 0:1, 0:48] = -2.0 * value_scale * weighting * margin
    gather_direct(VG, "vg", "vg")
    ready(l_no, l_gw, l_uw)
    gather_y(NO, "no", "no")
    GWT[...] = gw[...].T
    UWT[...] = uw[...].T

    for h, (lo, _, up) in enumerate(PARTS):
        t = pair_sum(0, h)
        came(("rf", h), RF.at[:, :, lo:up])
        for i in range(4):
            t = t + RF[i, :, lo:up].astype(F32)
        OWNH[:, lo:up] = t
        YS[:, lo:up] = t.astype(BF16)
        send(YS.at[:, lo:up], YR.at[:, lo:up], "y", ("y", h), ylp)

    gather_x(NO, "no", "no")

    def h_at(d):
        return k * 8 + zd(d)

    def h_send(name, a, lo, up, to):
        send(HA.at[a, :, lo:up], HA.at[a, :, lo:up], "ha", name, to)

    for h, (lo, _, up) in enumerate(PARTS):
        came(("y", h), YR.at[:, lo:up])
        HA[h_at(0), :, lo:up] = (OWNH[:, lo:up] + YR[:, lo:up].astype(F32)).astype(BF16)
        for d in (2, -2):
            h_send(("h", d, h), h_at(0), lo, up, zdev[d])
    for lo, _, up in PARTS:
        for d in (1, -1):
            h_send("h1", h_at(0), lo, up, zdev[d])

    def h_forward(name, *ds):
        for d in ds:
            send(HA.at[h_at(d)], HA.at[h_at(d)], "has", name, sib)

    h_forward("s0", 0)

    came("vg", VG.at[0:15])

    def out_grad(j, carry):
        VC[j] = jnp.broadcast_to(VG[j].T[:48, 0:1], (48, 128))
        wide = jnp.concatenate([VC[j]] * 2, axis=1)
        OG[j] = (GO[j].astype(F32) + wide * vw).astype(BF16)
        return carry

    lax.fori_loop(0, 16, out_grad, 0)
    came("guy", GU.at[1 - yl, :, k])
    send(GU.at[1 - yl, :, k], GU.at[1 - yl, :, k], "gus", "gus2", sib)

    for h, (lo, cut, up) in enumerate(PARTS):
        came(("h", 2, h), HA.at[h_at(-2), :, lo:up])
        h_send("h3", h_at(-2), lo, up, zdev[1])
        h_send("h4", h_at(-2), lo, cut, zdev[2])
        came(("h", -2, h), HA.at[h_at(2), :, lo:up])
        h_send("h3", h_at(2), lo, up, zdev[-1])
        h_send("h4", h_at(2), cut, up, zdev[-2])
    h_forward("s2", -2, 2)
    came("h1", HA.at[0:2])
    h_forward("s1", -1, 1)

    came("gus1", GU.at[yl, :, 1 - k])
    came("gus2", GU.at[1 - yl, :, 1 - k])

    def factors(j, carry):
        a = GU[j // 8, j % 8, 0].astype(F32)
        b = GU[j // 8, j % 8, 1].astype(F32)
        gate = jnp.concatenate([a[:24], b[:24]], axis=0)
        up = jnp.concatenate([a[24:], b[24:]], axis=0)
        s = jax.nn.sigmoid(gate)
        silu = gate * s
        SIL[j] = silu
        ACT[j] = (silu * up).astype(BF16)
        GF[j] = up * s * (1.0 + gate * (1.0 - s))
        return carry

    lax.fori_loop(0, 16, factors, 0)

    def tokens(name, *ds):
        if name is not None:
            came(name, HA.at[pl.ds(0, len(ds))])
        js = [j for d in ds for j in (k * 8 + zd(d), (1 - k) * 8 + zd(d))]
        for j in js:
            h = HA[j].astype(F32) + jnp.concatenate([VC[j]] * 7, axis=1) * U[...]
            GB[j] = (h * GF[j]).astype(BF16)
            UB[j] = (h * SIL[j]).astype(BF16)
        g = jnp.concatenate([GB[j] for j in js], axis=0)
        u = jnp.concatenate([UB[j] for j in js], axis=0)
        part = dot(g, GWT[...]) + dot(u, UWT[...])
        for i, j in enumerate(js):
            mine = part[48 * i : 48 * (i + 1)]
            CS[j] = mine.astype(BF16)

            @pl.when(j == col)
            def _():
                OWN[...] = mine

            @pl.when(j != col)
            def _():
                remote(CS.at[j], RIN.at[col], "cs", "cs", (row, j)).start()

    tokens("s0", 0)
    tokens("s2", -2, 2)
    tokens("s1", -1, 1)
    came("h3", HA.at[0:2])
    h_forward("s3", -3, 3)
    came("h4", HA.at[0])
    h_forward("s4", 4)
    tokens("s3", -3, 3)
    tokens("s4", 4)

    came("no", NO.at[0:12])
    NOT[...] = NO[...].reshape(768, 256).T
    o_gate[...] = dot(NOT[...], GB[...].reshape(768, 896)).astype(BF16)
    s_gate = load(o_gate, o_gate_h)
    o_up[...] = dot(NOT[...], UB[...].reshape(768, 896)).astype(BF16)
    s_up = load(o_up, o_up_h)
    o_down[...] = dot_tn(ACT[...].reshape(768, 896), OG[...].reshape(768, 256)).astype(BF16)
    s_down = load(o_down, o_down_h)

    left("go", GO.at[0:15])
    left("no", NO.at[0:15])
    left("vg", VG.at[0:15])
    left("guz", GU.at[0, 0:7, 0])
    left("guy", GU.at[0, :, 0])
    left("gus", GU.at[0])
    left("pk", PK)
    left("rs", SB.at[0:7])
    left("y", YS)
    left("ha", HA.at[0:7])
    left("has", HA.at[0:8])
    left("m0", M0)
    left("m1", M1)
    left("m2", MZ)

    remote(RIN.at[0:15], RIN.at[0:15], "cs", "cs", sib).wait()
    total = OWN[...]
    for i in range(1, 16):
        total = total + RIN[(col + i) % 16].astype(F32)
    o_normed[...] = total.astype(BF16)
    s_normed = load(o_normed, o_normed_h)
    for cp in (s_gate, s_up, s_down, s_normed):
        cp.wait()

def per_device(normed, gate_w, up_w, down_w, gate_pre, up_pre, block_out, value_w, q_target, grad_out):
    hbm = pl.BlockSpec(memory_space=pltpu.HBM)
    vmem = pl.BlockSpec(memory_space=pltpu.VMEM)
    scratch = [
        pltpu.VMEM((16, 48, 256), BF16),
        pltpu.VMEM((16, 48, 256), BF16),
        pltpu.VMEM((2, 8, 2, 48, 896), BF16),
        pltpu.VMEM((256, 896), BF16),
        pltpu.VMEM((256, 896), BF16),
        pltpu.VMEM((896, 256), BF16),
        pltpu.VMEM((896, 256), BF16),
        pltpu.VMEM((896, 256), BF16),
        pltpu.VMEM((256, 768), BF16),
        pltpu.VMEM((8, 48, 896), BF16),
        pltpu.VMEM((8, 48, 896), BF16),
        pltpu.VMEM((8, 48, 896), F32),
        pltpu.VMEM((8, 48, 896), BF16),
        pltpu.VMEM((48, 896), BF16),
        pltpu.VMEM((48, 896), BF16),
        pltpu.VMEM((48, 896), BF16),
        pltpu.VMEM((48, 896), BF16),
        pltpu.VMEM((4, 48, 896), BF16),
        pltpu.VMEM((48, 896), F32),
        pltpu.VMEM((48, 896), BF16),
        pltpu.VMEM((48, 896), BF16),
        pltpu.VMEM((16, 48, 896), BF16),
        pltpu.VMEM((16, 48, 896), F32),
        pltpu.VMEM((16, 48, 896), F32),
        pltpu.VMEM((16, 48, 896), BF16),
        pltpu.VMEM((16, 48, 896), BF16),
        pltpu.VMEM((16, 48, 896), BF16),
        pltpu.VMEM((16, 48, 256), BF16),
        pltpu.VMEM((16, 48, 256), BF16),
        pltpu.VMEM((16, 48, 256), BF16),
        pltpu.VMEM((48, 256), F32),
        pltpu.VMEM((48, 256), BF16),
        pltpu.VMEM((256, 896), BF16),
        pltpu.VMEM((256, 896), BF16),
        pltpu.VMEM((896, 256), BF16),
        pltpu.VMEM((8, 128), F32),
        pltpu.VMEM((8, 128), F32),
        pltpu.VMEM((8, 128), F32),
        pltpu.VMEM((8, 128), F32),
        pltpu.VMEM((8, 128), F32),
        pltpu.VMEM((7, 8, 128), F32),
        pltpu.VMEM((16, 8, 128), F32),
        pltpu.VMEM((16, 48, 128), F32),
        pltpu.VMEM((1, 896), F32),
        pltpu.SemaphoreType.DMA((N_LOCAL,)),
        pltpu.SemaphoreType.DMA((N_SEND,)),
        pltpu.SemaphoreType.DMA((N_RECV,)),
    ]
    outs = pl.pallas_call(
        kernel,
        out_shape=(
            jax.ShapeDtypeStruct((48, 256), BF16),
            jax.ShapeDtypeStruct((256, 896), BF16),
            jax.ShapeDtypeStruct((256, 896), BF16),
            jax.ShapeDtypeStruct((896, 256), BF16),
        ),
        in_specs=[hbm, hbm, hbm, hbm, vmem, vmem, vmem, vmem, vmem, hbm],
        out_specs=(hbm, hbm, hbm, hbm),
        scratch_shapes=scratch,
        compiler_params=pltpu.CompilerParams(
            collective_id=0, has_side_effects=True, vmem_limit_bytes=60 * 2**20
        ),
    )(
        normed, gate_w, up_w, down_w, gate_pre, up_pre, block_out,
        value_w.reshape(1, 256), q_target.reshape(1, 48), grad_out,
    )
    return outs

def solution(mesh):
    return jax.shard_map(
        per_device,
        mesh=mesh,
        in_specs=(
            P("col", "row"),
            P("row", "col"),
            P("row", "col"),
            P("col", "row"),
            P("row", "col"),
            P("row", "col"),
            P("col", "row"),
            P("row"),
            P("col"),
            P("col", "row"),
        ),
        out_specs=(P("col", "row"), P("row", "col"), P("row", "col"), P("col", "row")),
        check_vma=False,
    )
```

```python
import jax
import jax.numpy as jnp
from jax import lax
from jax.experimental import pallas as pl
from jax.experimental.pallas import tpu as pltpu
from jax.sharding import PartitionSpec as P

expectile = 0.7
value_scale = 8.0

F32 = jnp.float32
BF16 = jnp.bfloat16
MESH = pl.DeviceIdType.MESH

PARTS = ((0, 256, 512), (512, 640, 896))
CUT = 512
VMEM_BYTES = 60 * 2**20
N_SEND = 17
N_RECV = 47
N_LOCAL = 9

NT = (((1,), (1,)), ((), ()))
TN = (((0,), (0,)), ((), ()))


def dot_nt(a, b):
    return lax.dot_general(a, b, NT, preferred_element_type=F32)


def dot_tn(a, b):
    return lax.dot_general(a, b, TN, preferred_element_type=F32)


def dot(a, b):
    return jnp.dot(a, b, preferred_element_type=F32)


def kernel(
    normed_h, gate_w_h, up_w_h, down_w_h, gate_pre, up_pre, block_out, value_w, q_target, grad_out_h,
    o_normed_h, o_gate_h, o_up_h, o_down_h,
    GO, GOS, NO, GU, gw, uw, DW, GWT, UWT, NOT,
    KEEP, SB, RA1, RA2, RB1, RB2, RF, OWNH, YS, YR, HA,
    SIL, GF, ACT, GB, UB, OG,
    CS, RIN, OWN, o_normed, o_gate, o_up, o_down,
    M0, MS, M1, MY, M2, MZ, VG, VC, U,
    local, ss, rs,
):
    row, col = lax.axis_index("row"), lax.axis_index("col")
    k, z, yl = row % 2, (row // 2) % 8, row // 16
    x, yh = col % 4, col // 4

    def dev(k_=k, z_=z, yl_=yl, x_=x, yh_=yh):
        return ((yl_ * 8 + z_) * 2 + k_, yh_ * 4 + x_)

    def zd(d):
        return (z + d + 8) % 8

    def xd(d):
        return (x + d + 4) % 4

    def yd(d):
        return (yh + d + 4) % 4

    sib = dev(k_=1 - k)
    ylp = dev(yl_=1 - yl)
    zdev = {d: dev(z_=zd(d)) for d in (1, -1, 2, -2, 3, -3, 4)}
    xdev = {d: dev(x_=xd(d)) for d in (1, 2, 3)}
    ydev = {d: dev(yh_=yd(d)) for d in (1, 2, 3)}

    ids = {"send": {}, "recv": {}}
    loads = []

    def sem(side, name):
        known = ids[side]
        if name not in known:
            known[name] = len(known)
            assert len(known) <= (N_SEND if side == "send" else N_RECV)
        return (ss if side == "send" else rs).at[known[name]]

    def remote(src, dst, group, name, to):
        return pltpu.make_async_remote_copy(
            src, dst, sem("send", group), sem("recv", name), device_id=to, device_id_type=MESH
        )

    def send(src, dst, group, name, to):
        remote(src, dst, group, name, to).start()

    def came(name, ref):
        remote(ref, ref, "none", name, sib).wait_recv()

    def left(group, ref):
        remote(ref, ref, group, "none", sib).wait_send()

    def load(src, dst):
        cp = pltpu.make_async_copy(src, dst, local.at[len(loads)])
        cp.start()
        loads.append(cp)
        return cp

    def ready(*cps):
        for cp in cps:
            cp.wait()

    l_go = load(grad_out_h, GO.at[col])
    l_dw = load(down_w_h, DW.at[:, :256])
    l_no = load(normed_h, NO.at[col])
    l_gw = load(gate_w_h, gw)
    l_uw = load(up_w_h, uw)

    barrier = pltpu.get_barrier_semaphore()
    partners = [sib, ylp, *zdev.values()] + [(row, (col + i) % 16) for i in range(1, 16)]
    for p in partners:
        pl.semaphore_signal(barrier, inc=1, device_id=p, device_id_type=MESH)

    GU[yl, z, k] = jnp.concatenate([gate_pre[...].astype(F32), up_pre[...].astype(F32)], axis=0).astype(BF16)
    ready(l_go)
    pl.semaphore_wait(barrier, len(partners))

    def gather_direct(buf, group, name):
        for i in (10, 6, 14, 2, 9, 11, 5, 7, 13, 15, 1, 3, 8, 4, 12):
            send(buf.at[col], buf.at[col], group, name, (row, (col + i) % 16))

    def gather_y(buf, group, name):
        for d in (2, 1, 3):
            send(buf.at[col], buf.at[col], group, name if d == 2 else name + str(d), ydev[d])
        for d in (2, 1, 3):
            send(buf.at[col], buf.at[col], group, name, dev(x_=xd(d), yh_=yd(2)))
        for d in (2, 1, 3):
            send(buf.at[col], buf.at[col], group, name, xdev[d])

    def gather_x(buf, group, name):
        for dy in (1, 3):
            at = yd(-dy) * 4 + x
            came(name + str(dy), buf.at[at])
            for d in (2, 1, 3):
                send(buf.at[at], buf.at[at], group, name, xdev[d])

    gather_y(GO, "go", "go")

    def gu(d):
        return GU.at[yl, zd(d), k]

    def gu_y(d):
        send(gu(d), gu(d), "guy", "guy", ylp)

    for d, name in ((2, "gu+2"), (-2, "gu-2"), (1, "gu1"), (-1, "gu1")):
        send(gu(0), gu(0), "guz", name, zdev[d])
    gu_y(0)

    ready(l_dw)
    vw = value_w[...]
    hi = vw.astype(BF16).astype(F32)
    mid = (vw - hi).astype(BF16).astype(F32)
    lo = vw - hi - mid
    terms = jnp.concatenate([hi, mid, lo, jnp.zeros((5, 256), F32)], axis=0).astype(BF16)
    send(DW.at[:, :256], DW.at[:, 256:], "dw", "dw", sib)
    u_part = jnp.sum(dot_nt(terms, DW[:, :256]), axis=0, keepdims=True)
    v_part = jnp.sum(dot_nt(terms, block_out[...]), axis=0, keepdims=True)
    M0[...] = jnp.zeros((8, 128), F32)
    for i in range(7):
        M0[i : i + 1, :] = u_part[:, 128 * i : 128 * (i + 1)]
    M0[7:8, 0:48] = v_part
    send(M0, MS, "m0", "m0", sib)

    gather_x(GO, "go", "go")

    came("m0", MS)
    M1[...] = M0[...] + MS[...]
    send(M1, MY, "m1", "m1", ylp)

    came("gu+2", gu(-2))
    send(gu(-2), gu(-2), "guz", "gu3", zdev[1])
    send(gu(-2).at[:, :CUT], gu(-2).at[:, :CUT], "guz", "gu3", zdev[2])
    came("gu-2", gu(2))
    send(gu(2), gu(2), "guz", "gu3", zdev[-1])
    send(gu(2).at[:, CUT:], gu(2).at[:, CUT:], "guz", "gu3", zdev[-2])

    came("m1", MY)
    M2[...] = M1[...] + MY[...]
    for i, d in enumerate((4, 3, -3, 2, -2, 1, -1)):
        send(M2, MZ.at[i], "m2", "m2", zdev[d])

    gu_y(-2)
    gu_y(2)
    came("go", GO.at[0:13])

    half = pl.ds((1 - k) * 8, 8)
    send(GO.at[half], GOS, "gos", "gos", sib)
    came("dw", DW.at[:, 256:])
    came("gos", GOS)
    slot = {d: i for i, d in enumerate((3, -3, 4, 2, -2, 1, -1))}

    def partial(ds, h):
        lo, _, up = PARTS[h]
        rows = [jnp.concatenate([GO[k * 8 + zd(d)], GOS[zd(d)]], axis=1) for d in ds]
        p = dot_nt(jnp.concatenate(rows, axis=0), DW[lo:up])
        return [p[48 * i : 48 * (i + 1)] for i in range(len(ds))]

    def rs_first(h):
        lo, cut, up = PARTS[h]
        for d, p in zip((3, -3, 4, 2), partial((3, -3, 4, 2), h)):
            if d == 2:
                KEEP[1, :, lo:up] = p
                continue
            SB[slot[d], :, lo:up] = p.astype(BF16)
            src = SB.at[slot[d]]
            if d == 3:
                send(src.at[:, lo:up], RA1.at[:, lo:up], "rs", ("a1", h), zdev[1])
            elif d == -3:
                send(src.at[:, lo:up], RB1.at[:, lo:up], "rs", ("b1", h), zdev[-1])
            else:
                send(src.at[:, lo:cut], RA2.at[:, lo:cut], "rs", ("a2", h), zdev[2])
                send(src.at[:, cut:up], RB2.at[:, cut:up], "rs", ("b2", h), zdev[-2])

    def rs_near(h):
        lo, cut, up = PARTS[h]
        p = partial((1, -1, -2, 0), h)
        for i, d in enumerate((1, -1)):
            SB[slot[d], :, lo:up] = p[i].astype(BF16)
            send(SB.at[slot[d], :, lo:up], RF.at[i, :, lo:up], "rs", ("rf", h), zdev[d])
        KEEP[2, :, lo:up] = p[2]
        KEEP[0, :, lo:up] = p[3]

    def rs_second(h):
        lo, cut, up = PARTS[h]
        t = KEEP[1, :, lo:up]
        came(("a1", h), RA1.at[:, lo:up])
        came(("a2", h), RA2.at[:, lo:cut])
        t = t + RA1[:, lo:up].astype(F32)
        SB[slot[2], :, lo:cut] = (t[:, : cut - lo] + RA2[:, lo:cut].astype(F32)).astype(BF16)
        SB[slot[2], :, cut:up] = t[:, cut - lo :].astype(BF16)
        send(SB.at[slot[2], :, lo:up], RF.at[2, :, lo:up], "rs", ("rf", h), zdev[2])
        t = KEEP[2, :, lo:up]
        came(("b1", h), RB1.at[:, lo:up])
        came(("b2", h), RB2.at[:, cut:up])
        t = t + RB1[:, lo:up].astype(F32)
        SB[slot[-2], :, lo:cut] = t[:, : cut - lo].astype(BF16)
        SB[slot[-2], :, cut:up] = (t[:, cut - lo :] + RB2[:, cut:up].astype(F32)).astype(BF16)
        send(SB.at[slot[-2], :, lo:up], RF.at[3, :, lo:up], "rs", ("rf", h), zdev[-2])

    rs_first(0)
    rs_first(1)
    rs_near(0)
    came("gu1", GU.at[0, 0:2, 0])
    gu_y(-1)
    gu_y(1)
    rs_second(0)
    rs_near(1)
    rs_second(1)
    came("gu3", GU.at[0, 0:3, 0])
    for d in (-3, 3, 4):
        gu_y(d)

    send(GU.at[yl, :, k], GU.at[yl, :, k], "gus", "gus1", sib)
    came("m2", MZ)
    total = M2[...]
    for i in range(7):
        total = total + MZ[i]
    for i in range(7):
        U[:, 128 * i : 128 * (i + 1)] = total[i : i + 1, :]
    margin = q_target[...] - total[7:8, 0:48]
    weighting = jnp.where(margin > 0, expectile, 1.0 - expectile)
    VG[col] = jnp.zeros((8, 128), F32)
    VG[col, 0:1, 0:48] = -2.0 * value_scale * weighting * margin
    gather_direct(VG, "vg", "vg")

    for h, (lo, _, up) in enumerate(PARTS):
        t = KEEP[0, :, lo:up]
        came(("rf", h), RF.at[:, :, lo:up])
        for i in range(4):
            t = t + RF[i, :, lo:up].astype(F32)
        OWNH[:, lo:up] = t
        YS[:, lo:up] = t.astype(BF16)
        send(YS.at[:, lo:up], YR.at[:, lo:up], "y", ("y", h), ylp)

    ready(l_no, l_gw, l_uw)
    gather_y(NO, "no", "no")
    GWT[...] = gw[...].T
    UWT[...] = uw[...].T

    def h_at(d):
        return k * 8 + zd(d)

    def h_send(name, a, lo, up, to):
        send(HA.at[a, :, lo:up], HA.at[a, :, lo:up], "ha", name, to)

    for h, (lo, _, up) in enumerate(PARTS):
        came(("y", h), YR.at[:, lo:up])
        HA[h_at(0), :, lo:up] = (OWNH[:, lo:up] + YR[:, lo:up].astype(F32)).astype(BF16)
        for d in (2, -2):
            h_send(("h", d, h), h_at(0), lo, up, zdev[d])
    for lo, _, up in PARTS:
        for d in (1, -1):
            h_send("h1", h_at(0), lo, up, zdev[d])

    def h_forward(name, *ds):
        for d in ds:
            send(HA.at[h_at(d)], HA.at[h_at(d)], "has", name, sib)

    h_forward("s0", 0)
    gather_x(NO, "no", "no")

    came("vg", VG.at[0:15])

    def out_grad(j, carry):
        VC[j] = jnp.broadcast_to(VG[j].T[:48, 0:1], (48, 128))
        wide = jnp.concatenate([VC[j]] * 2, axis=1)
        OG[j] = (GO[j].astype(F32) + wide * vw).astype(BF16)
        return carry

    lax.fori_loop(0, 16, out_grad, 0, unroll=4)
    came("guy", GU.at[1 - yl, :, k])
    send(GU.at[1 - yl, :, k], GU.at[1 - yl, :, k], "gus", "gus2", sib)

    for h, (lo, cut, up) in enumerate(PARTS):
        came(("h", 2, h), HA.at[h_at(-2), :, lo:up])
        h_send("h3", h_at(-2), lo, up, zdev[1])
        h_send("h4", h_at(-2), lo, cut, zdev[2])
        came(("h", -2, h), HA.at[h_at(2), :, lo:up])
        h_send("h3", h_at(2), lo, up, zdev[-1])
        h_send("h4", h_at(2), cut, up, zdev[-2])
    h_forward("s2", -2, 2)
    came("h1", HA.at[0:2])
    h_forward("s1", -1, 1)

    came("gus1", GU.at[yl, :, 1 - k])
    came("gus2", GU.at[1 - yl, :, 1 - k])

    def factors(j, carry):
        a = GU[j // 8, j % 8, 0].astype(F32)
        b = GU[j // 8, j % 8, 1].astype(F32)
        gate = jnp.concatenate([a[:24], b[:24]], axis=0)
        up = jnp.concatenate([a[24:], b[24:]], axis=0)
        s = jax.nn.sigmoid(gate)
        silu = gate * s
        SIL[j] = silu
        ACT[j] = (silu * up).astype(BF16)
        GF[j] = up * s * (1.0 + gate * (1.0 - s))
        return carry

    lax.fori_loop(0, 16, factors, 0)

    def tokens(name, *ds):
        if name is not None:
            came(name, HA.at[pl.ds(0, len(ds))])
        js = [j for d in ds for j in (k * 8 + zd(d), (1 - k) * 8 + zd(d))]
        for j in js:
            h = HA[j].astype(F32) + jnp.concatenate([VC[j]] * 7, axis=1) * U[...]
            GB[j] = (h * GF[j]).astype(BF16)
            UB[j] = (h * SIL[j]).astype(BF16)
        g = jnp.concatenate([GB[j] for j in js], axis=0)
        u = jnp.concatenate([UB[j] for j in js], axis=0)
        part = dot(g, GWT[...]) + dot(u, UWT[...])
        for i, j in enumerate(js):
            mine = part[48 * i : 48 * (i + 1)]
            CS[j] = mine.astype(BF16)

            @pl.when(j == col)
            def _():
                OWN[...] = mine

            @pl.when(j != col)
            def _():
                remote(CS.at[j], RIN.at[col], "cs", "cs", (row, j)).start()

    tokens("s0", 0)
    tokens("s2", -2, 2)
    tokens("s1", -1, 1)
    o_down[...] = dot_tn(ACT[...].reshape(768, 896), OG[...].reshape(768, 256)).astype(BF16)
    s_down = load(o_down, o_down_h)
    came("h3", HA.at[0:2])
    h_forward("s3", -3, 3)
    came("h4", HA.at[0])
    h_forward("s4", 4)
    tokens("s3", -3, 3)
    tokens("s4", 4)

    came("no", NO.at[0:13])
    NOT[...] = NO[...].reshape(768, 256).T
    o_gate[...] = dot(NOT[...], GB[...].reshape(768, 896)).astype(BF16)
    s_gate = load(o_gate, o_gate_h)
    o_up[...] = dot(NOT[...], UB[...].reshape(768, 896)).astype(BF16)
    s_up = load(o_up, o_up_h)

    left("go", GO.at[0:15])
    left("no", NO.at[0:15])
    left("vg", VG.at[0:15])
    left("guz", GU.at[0, 0:7, 0])
    left("guy", GU.at[0, :, 0])
    left("gus", GU.at[0])
    left("gos", GOS)
    left("dw", DW.at[:, 256:])
    left("rs", SB.at[0:7])
    left("y", YS)
    left("ha", HA.at[0:7])
    left("has", HA.at[0:8])
    left("m0", M0)
    left("m1", M1)
    left("m2", MZ)

    remote(RIN.at[0:15], RIN.at[0:15], "cs", "cs", sib).wait()
    total = OWN[...]
    for i in range(1, 16):
        total = total + RIN[(col + i) % 16].astype(F32)
    o_normed[...] = total.astype(BF16)
    s_normed = load(o_normed, o_normed_h)
    for cp in (s_gate, s_up, s_down, s_normed):
        cp.wait()


def per_device(normed, gate_w, up_w, down_w, gate_pre, up_pre, block_out, value_w, q_target, grad_out):
    hbm = pl.BlockSpec(memory_space=pltpu.HBM)
    vmem = pl.BlockSpec(memory_space=pltpu.VMEM)
    scratch = [
        pltpu.VMEM((16, 48, 256), BF16),
        pltpu.VMEM((8, 48, 256), BF16),
        pltpu.VMEM((16, 48, 256), BF16),
        pltpu.VMEM((2, 8, 2, 48, 896), BF16),
        pltpu.VMEM((256, 896), BF16),
        pltpu.VMEM((256, 896), BF16),
        pltpu.VMEM((896, 512), BF16),
        pltpu.VMEM((896, 256), BF16),
        pltpu.VMEM((896, 256), BF16),
        pltpu.VMEM((256, 768), BF16),
        pltpu.VMEM((3, 48, 896), F32),
        pltpu.VMEM((8, 48, 896), BF16),
        pltpu.VMEM((48, 896), BF16),
        pltpu.VMEM((48, 896), BF16),
        pltpu.VMEM((48, 896), BF16),
        pltpu.VMEM((48, 896), BF16),
        pltpu.VMEM((4, 48, 896), BF16),
        pltpu.VMEM((48, 896), F32),
        pltpu.VMEM((48, 896), BF16),
        pltpu.VMEM((48, 896), BF16),
        pltpu.VMEM((16, 48, 896), BF16),
        pltpu.VMEM((16, 48, 896), F32),
        pltpu.VMEM((16, 48, 896), F32),
        pltpu.VMEM((16, 48, 896), BF16),
        pltpu.VMEM((16, 48, 896), BF16),
        pltpu.VMEM((16, 48, 896), BF16),
        pltpu.VMEM((16, 48, 256), BF16),
        pltpu.VMEM((16, 48, 256), BF16),
        pltpu.VMEM((16, 48, 256), BF16),
        pltpu.VMEM((48, 256), F32),
        pltpu.VMEM((48, 256), BF16),
        pltpu.VMEM((256, 896), BF16),
        pltpu.VMEM((256, 896), BF16),
        pltpu.VMEM((896, 256), BF16),
        pltpu.VMEM((8, 128), F32),
        pltpu.VMEM((8, 128), F32),
        pltpu.VMEM((8, 128), F32),
        pltpu.VMEM((8, 128), F32),
        pltpu.VMEM((8, 128), F32),
        pltpu.VMEM((7, 8, 128), F32),
        pltpu.VMEM((16, 8, 128), F32),
        pltpu.VMEM((16, 48, 128), F32),
        pltpu.VMEM((1, 896), F32),
        pltpu.SemaphoreType.DMA((N_LOCAL,)),
        pltpu.SemaphoreType.DMA((N_SEND,)),
        pltpu.SemaphoreType.DMA((N_RECV,)),
    ]
    outs = pl.pallas_call(
        kernel,
        out_shape=(
            jax.ShapeDtypeStruct((48, 256), BF16),
            jax.ShapeDtypeStruct((256, 896), BF16),
            jax.ShapeDtypeStruct((256, 896), BF16),
            jax.ShapeDtypeStruct((896, 256), BF16),
        ),
        in_specs=[hbm, hbm, hbm, hbm, vmem, vmem, vmem, vmem, vmem, hbm],
        out_specs=(hbm, hbm, hbm, hbm),
        scratch_shapes=scratch,
        compiler_params=pltpu.CompilerParams(
            collective_id=0, has_side_effects=True, vmem_limit_bytes=VMEM_BYTES
        ),
    )(
        normed, gate_w, up_w, down_w, gate_pre, up_pre, block_out,
        value_w.reshape(1, 256), q_target.reshape(1, 48), grad_out,
    )
    return pl.pallas_call(
        hand_over,
        out_shape=tuple(jax.ShapeDtypeStruct(o.shape, o.dtype) for o in outs),
        in_specs=[hbm] * 4,
        out_specs=(hbm,) * 4,
        scratch_shapes=[pltpu.VMEM(o.shape, o.dtype) for o in outs]
        + [pltpu.SemaphoreType.DMA((4,)), pltpu.SemaphoreType.DMA((4,))],
        compiler_params=pltpu.CompilerParams(vmem_limit_bytes=VMEM_BYTES),
    )(*outs)


def hand_over(a, b, c, d, oa, ob, oc, od, va, vb, vc, vd, s_in, s_out):
    four = range(4)
    ins = [pltpu.make_async_copy((a, b, c, d)[i], (va, vb, vc, vd)[i], s_in.at[i]) for i in four]
    outs = [pltpu.make_async_copy((va, vb, vc, vd)[i], (oa, ob, oc, od)[i], s_out.at[i]) for i in four]
    for cp in ins:
        cp.start()
    for i in four:
        ins[i].wait()
        outs[i].start()
    for cp in outs:
        cp.wait()


def solution(mesh):
    return jax.shard_map(
        per_device,
        mesh=mesh,
        in_specs=(
            P("col", "row"),
            P("row", "col"),
            P("row", "col"),
            P("col", "row"),
            P("row", "col"),
            P("row", "col"),
            P("col", "row"),
            P("row"),
            P("col"),
            P("col", "row"),
        ),
        out_specs=(P("col", "row"), P("row", "col"), P("row", "col"), P("col", "row")),
        check_vma=False,
    )
```

```python
import jax
import jax.numpy as jnp
from jax import lax
from jax.experimental import pallas as pl
from jax.experimental.pallas import tpu as pltpu
from jax.sharding import PartitionSpec as P

expectile = 0.7
value_scale = 8.0

F32 = jnp.float32
BF16 = jnp.bfloat16
MESH = pl.DeviceIdType.MESH

PARTS = ((0, 256, 512), (512, 640, 896))
CUT = 512
VMEM_BYTES = 60 * 2**20
N_SEND = 18
N_RECV = 50
N_LOCAL = 14

NT = (((1,), (1,)), ((), ()))
TN = (((0,), (0,)), ((), ()))


def dot_nt(a, b):
    return lax.dot_general(a, b, NT, preferred_element_type=F32)


def dot_tn(a, b):
    return lax.dot_general(a, b, TN, preferred_element_type=F32)


def dot(a, b):
    return jnp.dot(a, b, preferred_element_type=F32)


def kernel(
    normed_h, gate_w_h, up_w_h, down_w_h, gate_pre_h, up_pre_h, block_out_h, value_w_h, q_target_h, grad_out_h,
    o_normed_h, o_gate_h, o_up_h, o_down_h,
    GO, GOS, NO, GU, gw, uw, DW, DWT, GWT, UWT, NOT,
    KEEP, SB, RA1, RA2, RB1, RB2, RF, OWNH, YS, YR, HA,
    SIL, GF, ACT, GB, UB, OG,
    CS, RIN, OWN, o_normed, o_gate, o_up, o_down,
    gate_pre, up_pre, block_out, value_w, q_target, M0, MS, M1, MY, M2, MZ, VG, VC, U,
    local, ss, rs,
):
    row, col = lax.axis_index("row"), lax.axis_index("col")
    k, z, yl = row % 2, (row // 2) % 8, row // 16
    x, yh = col % 4, col // 4

    def dev(k_=k, z_=z, yl_=yl, x_=x, yh_=yh):
        return ((yl_ * 8 + z_) * 2 + k_, yh_ * 4 + x_)

    def zd(d):
        return (z + d + 8) % 8

    def xd(d):
        return (x + d + 4) % 4

    def yd(d):
        return (yh + d + 4) % 4

    sib = dev(k_=1 - k)
    ylp = dev(yl_=1 - yl)
    zdev = {d: dev(z_=zd(d)) for d in (1, -1, 2, -2, 3, -3, 4)}
    xdev = {d: dev(x_=xd(d)) for d in (1, 2, 3)}
    ydev = {d: dev(yh_=yd(d)) for d in (1, 2, 3)}

    ids = {"send": {}, "recv": {}}
    loads = []

    def sem(side, name):
        known = ids[side]
        if name not in known:
            known[name] = len(known)
            assert len(known) <= (N_SEND if side == "send" else N_RECV)
        return (ss if side == "send" else rs).at[known[name]]

    def remote(src, dst, group, name, to):
        return pltpu.make_async_remote_copy(
            src, dst, sem("send", group), sem("recv", name), device_id=to, device_id_type=MESH
        )

    def send(src, dst, group, name, to):
        remote(src, dst, group, name, to).start()

    def came(name, ref):
        remote(ref, ref, "none", name, sib).wait_recv()

    def left(group, ref):
        remote(ref, ref, group, "none", sib).wait_send()

    def load(src, dst):
        cp = pltpu.make_async_copy(src, dst, local.at[len(loads)])
        cp.start()
        loads.append(cp)
        return cp

    def ready(*cps):
        for cp in cps:
            cp.wait()

    barrier = pltpu.get_barrier_semaphore()
    partners = [sib, ylp, *zdev.values()] + [(row, (col + i) % 16) for i in range(1, 16)]
    for p in partners:
        pl.semaphore_signal(barrier, inc=1, device_id=p, device_id_type=MESH)

    l_go = load(grad_out_h, GO.at[col])
    l_gu = load(gate_pre_h, gate_pre), load(up_pre_h, up_pre)
    l_v = load(block_out_h, block_out), load(value_w_h, value_w), load(q_target_h, q_target)
    l_dw = load(down_w_h, DW.at[:, :256])
    l_no = load(normed_h, NO.at[col])
    l_gw = load(gate_w_h, gw)
    l_uw = load(up_w_h, uw)
    ready(l_go, *l_gu)
    GU[yl, z, k] = jnp.concatenate([gate_pre[...].astype(F32), up_pre[...].astype(F32)], axis=0).astype(BF16)
    pl.semaphore_wait(barrier, len(partners))

    def gather_direct(buf, group, name):
        for i in (10, 6, 14, 2, 9, 11, 5, 7, 13, 15, 1, 3, 8, 4, 12):
            send(buf.at[col], buf.at[col], group, name, (row, (col + i) % 16))

    def gather_y(buf, group, name):
        for d in (2, 1, 3):
            send(buf.at[col], buf.at[col], group, name + str(d), ydev[d])
        for d in (2, 1, 3):
            send(buf.at[col], buf.at[col], group, name, xdev[d])

    def gather_x(buf, group, name):
        for dy in (1, 3, 2):
            at = yd(-dy) * 4 + x
            came(name + str(dy), buf.at[at])
            for d in (2, 1, 3):
                send(buf.at[at], buf.at[at], group, name, xdev[d])

    gather_y(GO, "go", "go")

    def gu(d):
        return GU.at[yl, zd(d), k]

    def gu_y(d):
        send(gu(d), gu(d), "guy", "guy" if d else "gp0", ylp)

    for d, name in ((2, "gu+2"), (-2, "gu-2"), (1, "gu1"), (-1, "gu1")):
        send(gu(0), gu(0), "guz", name, zdev[d])
    gu_y(0)

    ready(l_dw, *l_v)
    vw = value_w[...]
    hi = vw.astype(BF16).astype(F32)
    mid = (vw - hi).astype(BF16).astype(F32)
    lo = vw - hi - mid
    terms = jnp.concatenate([hi, mid, lo, jnp.zeros((5, 256), F32)], axis=0).astype(BF16)
    send(DW.at[:, :256], DW.at[:, 256:], "dw", "dw", sib)
    u_part = jnp.sum(dot_nt(terms, DW[:, :256]), axis=0, keepdims=True)
    v_part = jnp.sum(dot_nt(terms, block_out[...]), axis=0, keepdims=True)
    M0[...] = jnp.zeros((8, 128), F32)
    for i in range(7):
        M0[i : i + 1, :] = u_part[:, 128 * i : 128 * (i + 1)]
    M0[7:8, 0:48] = v_part
    send(M0, MS, "m0", "m0", sib)

    gather_x(GO, "go", "go")

    came("m0", MS)
    M1[...] = M0[...] + MS[...]
    send(M1, MY, "m1", "m1", ylp)

    pair = GU.at[1 - yl, z, k]
    came("gp0", pair)
    for d in (1, -1):
        send(pair, pair, "gp", "gp1", zdev[d])
    came("gu+2", gu(-2))
    send(gu(-2), gu(-2), "guz", "gu3", zdev[1])
    send(gu(-2).at[:, :CUT], gu(-2).at[:, :CUT], "guz", "gu3", zdev[2])
    came("gu-2", gu(2))
    send(gu(2), gu(2), "guz", "gu3", zdev[-1])
    send(gu(2).at[:, CUT:], gu(2).at[:, CUT:], "guz", "gu3", zdev[-2])

    came("m1", MY)
    M2[...] = M1[...] + MY[...]
    for i, d in enumerate((4, 3, -3, 2, -2, 1, -1)):
        send(M2, MZ.at[i], "m2", "m2", zdev[d])

    gu_y(-2)
    gu_y(2)
    came("dw", DW.at[:, 256:])
    DWT[...] = DW[...].T
    came("go", GO.at[0:12])

    half = pl.ds((1 - k) * 8, 8)
    send(GO.at[half], GOS, "gos", "gos", sib)
    came("gos", GOS)
    slot = {d: i for i, d in enumerate((3, -3, 4, 2, -2, 1, -1))}

    def partial(ds, h):
        lo, _, up = PARTS[h]
        rows = [jnp.concatenate([GO[k * 8 + zd(d)], GOS[zd(d)]], axis=1) for d in ds]
        p = dot(jnp.concatenate(rows, axis=0), DWT[:, lo:up])
        return [p[48 * i : 48 * (i + 1)] for i in range(len(ds))]

    def rs_first(h):
        lo, cut, up = PARTS[h]
        for d, p in zip((3, -3, 4, 2), partial((3, -3, 4, 2), h)):
            if d == 2:
                KEEP[1, :, lo:up] = p
                continue
            SB[slot[d], :, lo:up] = p.astype(BF16)
            src = SB.at[slot[d]]
            if d == 3:
                send(src.at[:, lo:up], RA1.at[:, lo:up], "rs", ("a1", h), zdev[1])
            elif d == -3:
                send(src.at[:, lo:up], RB1.at[:, lo:up], "rs", ("b1", h), zdev[-1])
            else:
                send(src.at[:, lo:cut], RA2.at[:, lo:cut], "rs", ("a2", h), zdev[2])
                send(src.at[:, cut:up], RB2.at[:, cut:up], "rs", ("b2", h), zdev[-2])

    def rs_near(h):
        lo, cut, up = PARTS[h]
        p = partial((1, -1, -2, 0), h)
        for i, d in enumerate((1, -1)):
            SB[slot[d], :, lo:up] = p[i].astype(BF16)
            send(SB.at[slot[d], :, lo:up], RF.at[i, :, lo:up], "rs", ("rf", h), zdev[d])
        KEEP[2, :, lo:up] = p[2]
        KEEP[0, :, lo:up] = p[3]

    def rs_second(h):
        lo, cut, up = PARTS[h]
        t = KEEP[1, :, lo:up]
        came(("a1", h), RA1.at[:, lo:up])
        came(("a2", h), RA2.at[:, lo:cut])
        t = t + RA1[:, lo:up].astype(F32)
        SB[slot[2], :, lo:cut] = (t[:, : cut - lo] + RA2[:, lo:cut].astype(F32)).astype(BF16)
        SB[slot[2], :, cut:up] = t[:, cut - lo :].astype(BF16)
        send(SB.at[slot[2], :, lo:up], RF.at[2, :, lo:up], "rs", ("rf", h), zdev[2])
        t = KEEP[2, :, lo:up]
        came(("b1", h), RB1.at[:, lo:up])
        came(("b2", h), RB2.at[:, cut:up])
        t = t + RB1[:, lo:up].astype(F32)
        SB[slot[-2], :, lo:cut] = t[:, : cut - lo].astype(BF16)
        SB[slot[-2], :, cut:up] = (t[:, cut - lo :] + RB2[:, cut:up].astype(F32)).astype(BF16)
        send(SB.at[slot[-2], :, lo:up], RF.at[3, :, lo:up], "rs", ("rf", h), zdev[-2])

    rs_first(0)
    rs_first(1)
    rs_near(0)
    came("m2", MZ)
    total = M2[...]
    for i in range(7):
        total = total + MZ[i]
    for i in range(7):
        U[:, 128 * i : 128 * (i + 1)] = total[i : i + 1, :]
    margin = q_target[...] - total[7:8, 0:48]
    weighting = jnp.where(margin > 0, expectile, 1.0 - expectile)
    VG[col] = jnp.zeros((8, 128), F32)
    VG[col, 0:1, 0:48] = -2.0 * value_scale * weighting * margin
    gather_direct(VG, "vg", "vg")
    rs_second(0)
    rs_near(1)
    rs_second(1)
    came("gu1", GU.at[0, 0:2, 0])
    came("gu3", GU.at[0, 0:3, 0])
    for d in (-3, 3, 4):
        gu_y(d)

    send(GU.at[yl, :, k], GU.at[yl, :, k], "gus", "gus1", sib)
    for h, (lo, _, up) in enumerate(PARTS):
        t = KEEP[0, :, lo:up]
        came(("rf", h), RF.at[:, :, lo:up])
        for i in range(4):
            t = t + RF[i, :, lo:up].astype(F32)
        OWNH[:, lo:up] = t
        YS[:, lo:up] = t.astype(BF16)
        send(YS.at[:, lo:up], YR.at[:, lo:up], "y", ("y", h), ylp)

    ready(l_no, l_gw, l_uw)
    GWT[...] = gw[...].T
    UWT[...] = uw[...].T

    came("gp1", GU.at[0, 0:2, 0])
    came("guy", GU.at[0, 0:5, 0])
    send(GU.at[1 - yl, :, k], GU.at[1 - yl, :, k], "gus", "gus2", sib)
    gather_y(NO, "no", "no")

    def h_at(d):
        return k * 8 + zd(d)

    def h_send(name, a, lo, up, to):
        send(HA.at[a, :, lo:up], HA.at[a, :, lo:up], "ha", name, to)

    for h, (lo, _, up) in enumerate(PARTS):
        came(("y", h), YR.at[:, lo:up])
        HA[h_at(0), :, lo:up] = (OWNH[:, lo:up] + YR[:, lo:up].astype(F32)).astype(BF16)
        for d in (2, -2):
            h_send(("h", d, h), h_at(0), lo, up, zdev[d])
    for lo, _, up in PARTS:
        for d in (1, -1):
            h_send("h1", h_at(0), lo, up, zdev[d])

    def h_forward(name, *ds):
        for d in ds:
            send(HA.at[h_at(d)], HA.at[h_at(d)], "has", name, sib)

    h_forward("s0", 0)

    came("vg", VG.at[0:15])

    def out_grad(j, carry):
        VC[j] = jnp.broadcast_to(VG[j].T[:48, 0:1], (48, 128))
        wide = jnp.concatenate([VC[j]] * 2, axis=1)
        OG[j] = (GO[j].astype(F32) + wide * vw).astype(BF16)
        return carry

    lax.fori_loop(0, 16, out_grad, 0, unroll=4)

    came("gus1", GU.at[yl, :, 1 - k])
    came("gus2", GU.at[1 - yl, :, 1 - k])

    def factors(j, carry):
        a = GU[j // 8, j % 8, 0].astype(F32)
        b = GU[j // 8, j % 8, 1].astype(F32)
        gate = jnp.concatenate([a[:24], b[:24]], axis=0)
        up = jnp.concatenate([a[24:], b[24:]], axis=0)
        s = jax.nn.sigmoid(gate)
        silu = gate * s
        SIL[j] = silu
        ACT[j] = (silu * up).astype(BF16)
        GF[j] = up * s * (1.0 + gate * (1.0 - s))
        return carry

    lax.fori_loop(0, 16, factors, 0)

    for h, (lo, cut, up) in enumerate(PARTS):
        came(("h", 2, h), HA.at[h_at(-2), :, lo:up])
        h_send("h3", h_at(-2), lo, up, zdev[1])
        h_send("h4", h_at(-2), lo, cut, zdev[2])
        came(("h", -2, h), HA.at[h_at(2), :, lo:up])
        h_send("h3", h_at(2), lo, up, zdev[-1])
        h_send("h4", h_at(2), cut, up, zdev[-2])
    h_forward("s2", -2, 2)
    came("h1", HA.at[0:2])
    h_forward("s1", -1, 1)

    gather_x(NO, "no", "no")
    def tokens(name, *ds):
        if name is not None:
            came(name, HA.at[pl.ds(0, len(ds))])
        js = [j for d in ds for j in (k * 8 + zd(d), (1 - k) * 8 + zd(d))]
        for j in js:
            h = HA[j].astype(F32) + jnp.concatenate([VC[j]] * 7, axis=1) * U[...]
            GB[j] = (h * GF[j]).astype(BF16)
            UB[j] = (h * SIL[j]).astype(BF16)
        g = jnp.concatenate([GB[j] for j in js], axis=0)
        u = jnp.concatenate([UB[j] for j in js], axis=0)
        part = dot(g, GWT[...]) + dot(u, UWT[...])
        for i, j in enumerate(js):
            mine = part[48 * i : 48 * (i + 1)]
            CS[j] = mine.astype(BF16)

            @pl.when(j == col)
            def _():
                OWN[...] = mine

            @pl.when(j != col)
            def _():
                remote(CS.at[j], RIN.at[col], "cs", "cs", (row, j)).start()

    tokens("s0", 0)
    tokens("s2", -2, 2)
    tokens("s1", -1, 1)
    o_down[...] = dot_tn(ACT[...].reshape(768, 896), OG[...].reshape(768, 256)).astype(BF16)
    s_down = load(o_down, o_down_h)
    came("h3", HA.at[0:2])
    h_forward("s3", -3, 3)
    came("h4", HA.at[0])
    h_forward("s4", 4)
    tokens("s3", -3, 3)
    tokens("s4", 4)

    came("no", NO.at[0:12])
    NOT[...] = NO[...].reshape(768, 256).T
    o_gate[...] = dot(NOT[...], GB[...].reshape(768, 896)).astype(BF16)
    s_gate = load(o_gate, o_gate_h)
    o_up[...] = dot(NOT[...], UB[...].reshape(768, 896)).astype(BF16)
    s_up = load(o_up, o_up_h)

    left("go", GO.at[0:15])
    left("no", NO.at[0:15])
    left("vg", VG.at[0:15])
    left("guz", GU.at[0, 0:7, 0])
    left("gp", GU.at[0, 0:2, 0])
    left("guy", GU.at[0, 0:6, 0])
    left("gus", GU.at[0])
    left("gos", GOS)
    left("dw", DW.at[:, 256:])
    left("rs", SB.at[0:7])
    left("y", YS)
    left("ha", HA.at[0:7])
    left("has", HA.at[0:8])
    left("m0", M0)
    left("m1", M1)
    left("m2", MZ)

    remote(RIN.at[0:15], RIN.at[0:15], "cs", "cs", sib).wait()
    total = OWN[...]
    for i in range(1, 16):
        total = total + RIN[(col + i) % 16].astype(F32)
    o_normed[...] = total.astype(BF16)
    s_normed = load(o_normed, o_normed_h)
    for cp in (s_gate, s_up, s_down, s_normed):
        cp.wait()


def per_device(normed, gate_w, up_w, down_w, gate_pre, up_pre, block_out, value_w, q_target, grad_out):
    hbm = pl.BlockSpec(memory_space=pltpu.HBM)
    scratch = [
        pltpu.VMEM((16, 48, 256), BF16),
        pltpu.VMEM((8, 48, 256), BF16),
        pltpu.VMEM((16, 48, 256), BF16),
        pltpu.VMEM((2, 8, 2, 48, 896), BF16),
        pltpu.VMEM((256, 896), BF16),
        pltpu.VMEM((256, 896), BF16),
        pltpu.VMEM((896, 512), BF16),
        pltpu.VMEM((512, 896), BF16),
        pltpu.VMEM((896, 256), BF16),
        pltpu.VMEM((896, 256), BF16),
        pltpu.VMEM((256, 768), BF16),
        pltpu.VMEM((3, 48, 896), F32),
        pltpu.VMEM((8, 48, 896), BF16),
        pltpu.VMEM((48, 896), BF16),
        pltpu.VMEM((48, 896), BF16),
        pltpu.VMEM((48, 896), BF16),
        pltpu.VMEM((48, 896), BF16),
        pltpu.VMEM((4, 48, 896), BF16),
        pltpu.VMEM((48, 896), F32),
        pltpu.VMEM((48, 896), BF16),
        pltpu.VMEM((48, 896), BF16),
        pltpu.VMEM((16, 48, 896), BF16),
        pltpu.VMEM((16, 48, 896), F32),
        pltpu.VMEM((16, 48, 896), F32),
        pltpu.VMEM((16, 48, 896), BF16),
        pltpu.VMEM((16, 48, 896), BF16),
        pltpu.VMEM((16, 48, 896), BF16),
        pltpu.VMEM((16, 48, 256), BF16),
        pltpu.VMEM((16, 48, 256), BF16),
        pltpu.VMEM((16, 48, 256), BF16),
        pltpu.VMEM((48, 256), F32),
        pltpu.VMEM((48, 256), BF16),
        pltpu.VMEM((256, 896), BF16),
        pltpu.VMEM((256, 896), BF16),
        pltpu.VMEM((896, 256), BF16),
        pltpu.VMEM((24, 896), BF16),
        pltpu.VMEM((24, 896), BF16),
        pltpu.VMEM((48, 256), BF16),
        pltpu.VMEM((1, 256), F32),
        pltpu.VMEM((1, 48), F32),
        pltpu.VMEM((8, 128), F32),
        pltpu.VMEM((8, 128), F32),
        pltpu.VMEM((8, 128), F32),
        pltpu.VMEM((8, 128), F32),
        pltpu.VMEM((8, 128), F32),
        pltpu.VMEM((7, 8, 128), F32),
        pltpu.VMEM((16, 8, 128), F32),
        pltpu.VMEM((16, 48, 128), F32),
        pltpu.VMEM((1, 896), F32),
        pltpu.SemaphoreType.DMA((N_LOCAL,)),
        pltpu.SemaphoreType.DMA((N_SEND,)),
        pltpu.SemaphoreType.DMA((N_RECV,)),
    ]
    outs = pl.pallas_call(
        kernel,
        out_shape=(
            jax.ShapeDtypeStruct((48, 256), BF16),
            jax.ShapeDtypeStruct((256, 896), BF16),
            jax.ShapeDtypeStruct((256, 896), BF16),
            jax.ShapeDtypeStruct((896, 256), BF16),
        ),
        in_specs=[hbm] * 10,
        out_specs=(hbm, hbm, hbm, hbm),
        scratch_shapes=scratch,
        compiler_params=pltpu.CompilerParams(
            collective_id=0, has_side_effects=True, vmem_limit_bytes=VMEM_BYTES
        ),
    )(
        normed, gate_w, up_w, down_w, gate_pre, up_pre, block_out,
        value_w.reshape(1, 256), q_target.reshape(1, 48), grad_out,
    )
    return pl.pallas_call(
        hand_over,
        out_shape=tuple(jax.ShapeDtypeStruct(o.shape, o.dtype) for o in outs),
        in_specs=[hbm] * 4,
        out_specs=(hbm,) * 4,
        scratch_shapes=[pltpu.VMEM(o.shape, o.dtype) for o in outs]
        + [pltpu.SemaphoreType.DMA((4,)), pltpu.SemaphoreType.DMA((4,))],
        compiler_params=pltpu.CompilerParams(vmem_limit_bytes=VMEM_BYTES),
    )(*outs)


def hand_over(a, b, c, d, oa, ob, oc, od, va, vb, vc, vd, s_in, s_out):
    four = range(4)
    ins = [pltpu.make_async_copy((a, b, c, d)[i], (va, vb, vc, vd)[i], s_in.at[i]) for i in four]
    outs = [pltpu.make_async_copy((va, vb, vc, vd)[i], (oa, ob, oc, od)[i], s_out.at[i]) for i in four]
    for cp in ins:
        cp.start()
    for i in four:
        ins[i].wait()
        outs[i].start()
    for cp in outs:
        cp.wait()


def solution(mesh):
    return jax.shard_map(
        per_device,
        mesh=mesh,
        in_specs=(
            P("col", "row"),
            P("row", "col"),
            P("row", "col"),
            P("col", "row"),
            P("row", "col"),
            P("row", "col"),
            P("col", "row"),
            P("row"),
            P("col"),
            P("col", "row"),
        ),
        out_specs=(P("col", "row"), P("row", "col"), P("row", "col"), P("col", "row")),
        check_vma=False,
    )
```

```python
import jax
import jax.numpy as jnp
from jax import lax
from jax.experimental import pallas as pl
from jax.experimental.pallas import tpu as pltpu
from jax.sharding import PartitionSpec as P

expectile = 0.7
value_scale = 8.0

F32 = jnp.float32
BF16 = jnp.bfloat16
MESH = pl.DeviceIdType.MESH

PARTS = ((0, 128, 256), (256, 384, 512), (512, 640, 896))
CUT = 512
VMEM_BYTES = 60 * 2**20
N_SEND = 18
N_RECV = 58
N_LOCAL = 14

NT = (((1,), (1,)), ((), ()))
TN = (((0,), (0,)), ((), ()))


def dot_nt(a, b):
    return lax.dot_general(a, b, NT, preferred_element_type=F32)


def dot_tn(a, b):
    return lax.dot_general(a, b, TN, preferred_element_type=F32)


def dot(a, b):
    return jnp.dot(a, b, preferred_element_type=F32)


def kernel(
    normed_h, gate_w_h, up_w_h, down_w_h, gate_pre_h, up_pre_h, block_out_h, value_w_h, q_target_h, grad_out_h,
    o_normed_h, o_gate_h, o_up_h, o_down_h,
    GO, GOS, NO, GU, gw, uw, DW, DWT, GWT, UWT, NOT,
    KEEP, SB, RA1, RA2, RB1, RB2, RF, OWNH, YS, YR, HA,
    SIL, GF, ACT, GB, UB, OG,
    CS, RIN, OWN, o_normed, o_gate, o_up, o_down,
    gate_pre, up_pre, block_out, value_w, q_target, M0, MS, M1, MY, M2, MZ, VG, VC, U,
    local, ss, rs,
):
    row, col = lax.axis_index("row"), lax.axis_index("col")
    k, z, yl = row % 2, (row // 2) % 8, row // 16
    x, yh = col % 4, col // 4

    def dev(k_=k, z_=z, yl_=yl, x_=x, yh_=yh):
        return ((yl_ * 8 + z_) * 2 + k_, yh_ * 4 + x_)

    def zd(d):
        return (z + d + 8) % 8

    def xd(d):
        return (x + d + 4) % 4

    def yd(d):
        return (yh + d + 4) % 4

    sib = dev(k_=1 - k)
    ylp = dev(yl_=1 - yl)
    zdev = {d: dev(z_=zd(d)) for d in (1, -1, 2, -2, 3, -3, 4)}
    xdev = {d: dev(x_=xd(d)) for d in (1, 2, 3)}
    ydev = {d: dev(yh_=yd(d)) for d in (1, 2, 3)}

    ids = {"send": {}, "recv": {}}
    loads = []

    def sem(side, name):
        known = ids[side]
        if name not in known:
            known[name] = len(known)
            assert len(known) <= (N_SEND if side == "send" else N_RECV)
        return (ss if side == "send" else rs).at[known[name]]

    def remote(src, dst, group, name, to):
        return pltpu.make_async_remote_copy(
            src, dst, sem("send", group), sem("recv", name), device_id=to, device_id_type=MESH
        )

    def send(src, dst, group, name, to):
        remote(src, dst, group, name, to).start()

    def came(name, ref):
        remote(ref, ref, "none", name, sib).wait_recv()

    def left(group, ref):
        remote(ref, ref, group, "none", sib).wait_send()

    def load(src, dst):
        cp = pltpu.make_async_copy(src, dst, local.at[len(loads)])
        cp.start()
        loads.append(cp)
        return cp

    def ready(*cps):
        for cp in cps:
            cp.wait()

    barrier = pltpu.get_barrier_semaphore()
    partners = [sib, ylp, *zdev.values()] + [(row, (col + i) % 16) for i in range(1, 16)]
    for p in partners:
        pl.semaphore_signal(barrier, inc=1, device_id=p, device_id_type=MESH)

    l_go = load(grad_out_h, GO.at[col])
    l_gu = load(gate_pre_h, gate_pre), load(up_pre_h, up_pre)
    l_v = load(block_out_h, block_out), load(value_w_h, value_w), load(q_target_h, q_target)
    l_dw = load(down_w_h, DW.at[:, :256])
    l_no = load(normed_h, NO.at[col])
    l_gw = load(gate_w_h, gw)
    l_uw = load(up_w_h, uw)
    ready(l_go, *l_gu)
    GU[yl, z, k] = jnp.concatenate([gate_pre[...].astype(F32), up_pre[...].astype(F32)], axis=0).astype(BF16)
    pl.semaphore_wait(barrier, len(partners))

    def gather_direct(buf, group, name):
        for i in (10, 6, 14, 2, 9, 11, 5, 7, 13, 15, 1, 3, 8, 4, 12):
            send(buf.at[col], buf.at[col], group, name, (row, (col + i) % 16))

    def gather_y(buf, group, name):
        for d in (2, 1, 3):
            send(buf.at[col], buf.at[col], group, name + str(d), ydev[d])
        for d in (2, 1, 3):
            send(buf.at[col], buf.at[col], group, name, xdev[d])

    def gather_x(buf, group, name):
        for dy in (1, 3, 2):
            at = yd(-dy) * 4 + x
            came(name + str(dy), buf.at[at])
            for d in (2, 1, 3):
                send(buf.at[at], buf.at[at], group, name, xdev[d])

    gather_y(GO, "go", "go")

    def gu(d):
        return GU.at[yl, zd(d), k]

    def gu_y(d):
        send(gu(d), gu(d), "guy", "guy" if d else "gp0", ylp)

    for d, name in ((2, "gu+2"), (-2, "gu-2"), (1, "gu1"), (-1, "gu1")):
        send(gu(0), gu(0), "guz", name, zdev[d])
    gu_y(0)

    ready(l_dw, *l_v)
    vw = value_w[...]
    hi = vw.astype(BF16).astype(F32)
    mid = (vw - hi).astype(BF16).astype(F32)
    lo = vw - hi - mid
    terms = jnp.concatenate([hi, mid, lo, jnp.zeros((5, 256), F32)], axis=0).astype(BF16)
    send(DW.at[:, :256], DW.at[:, 256:], "dw", "dw", sib)
    u_part = jnp.sum(dot_nt(terms, DW[:, :256]), axis=0, keepdims=True)
    v_part = jnp.sum(dot_nt(terms, block_out[...]), axis=0, keepdims=True)
    M0[...] = jnp.zeros((8, 128), F32)
    for i in range(7):
        M0[i : i + 1, :] = u_part[:, 128 * i : 128 * (i + 1)]
    M0[7:8, 0:48] = v_part
    send(M0, MS, "m0", "m0", sib)

    gather_x(GO, "go", "go")

    came("m0", MS)
    M1[...] = M0[...] + MS[...]
    send(M1, MY, "m1", "m1", ylp)

    pair = GU.at[1 - yl, z, k]
    came("gp0", pair)
    for d in (1, -1):
        send(pair, pair, "gp", "gp1", zdev[d])
    came("gu+2", gu(-2))
    send(gu(-2), gu(-2), "guz", "gu3", zdev[1])
    send(gu(-2).at[:, :CUT], gu(-2).at[:, :CUT], "guz", "gu3", zdev[2])
    came("gu-2", gu(2))
    send(gu(2), gu(2), "guz", "gu3", zdev[-1])
    send(gu(2).at[:, CUT:], gu(2).at[:, CUT:], "guz", "gu3", zdev[-2])

    came("m1", MY)
    M2[...] = M1[...] + MY[...]
    for i, d in enumerate((4, 3, -3, 2, -2, 1, -1)):
        send(M2, MZ.at[i], "m2", "m2", zdev[d])

    gu_y(-2)
    gu_y(2)
    came("dw", DW.at[:, 256:])
    DWT[...] = DW[...].T
    came("go", GO.at[0:12])

    half = pl.ds((1 - k) * 8, 8)
    send(GO.at[half], GOS, "gos", "gos", sib)
    came("gos", GOS)
    slot = {d: i for i, d in enumerate((3, -3, 4, 2, -2, 1, -1))}

    def partial(ds, h):
        lo, _, up = PARTS[h]
        rows = [jnp.concatenate([GO[k * 8 + zd(d)], GOS[zd(d)]], axis=1) for d in ds]
        p = dot(jnp.concatenate(rows, axis=0), DWT[:, lo:up])
        return [p[48 * i : 48 * (i + 1)] for i in range(len(ds))]

    def rs_first(h):
        lo, cut, up = PARTS[h]
        for d, p in zip((3, -3, 4, 2), partial((3, -3, 4, 2), h)):
            if d == 2:
                KEEP[1, :, lo:up] = p
                continue
            SB[slot[d], :, lo:up] = p.astype(BF16)
            src = SB.at[slot[d]]
            if d == 3:
                send(src.at[:, lo:up], RA1.at[:, lo:up], "rs", ("a1", h), zdev[1])
            elif d == -3:
                send(src.at[:, lo:up], RB1.at[:, lo:up], "rs", ("b1", h), zdev[-1])
            else:
                send(src.at[:, lo:cut], RA2.at[:, lo:cut], "rs", ("a2", h), zdev[2])
                send(src.at[:, cut:up], RB2.at[:, cut:up], "rs", ("b2", h), zdev[-2])

    def rs_near(h):
        lo, cut, up = PARTS[h]
        p = partial((1, -1, -2, 0), h)
        for i, d in enumerate((1, -1)):
            SB[slot[d], :, lo:up] = p[i].astype(BF16)
            send(SB.at[slot[d], :, lo:up], RF.at[i, :, lo:up], "rs", ("rf", h), zdev[d])
        KEEP[2, :, lo:up] = p[2]
        KEEP[0, :, lo:up] = p[3]

    def rs_second(h):
        lo, cut, up = PARTS[h]
        t = KEEP[1, :, lo:up]
        came(("a1", h), RA1.at[:, lo:up])
        came(("a2", h), RA2.at[:, lo:cut])
        t = t + RA1[:, lo:up].astype(F32)
        SB[slot[2], :, lo:cut] = (t[:, : cut - lo] + RA2[:, lo:cut].astype(F32)).astype(BF16)
        SB[slot[2], :, cut:up] = t[:, cut - lo :].astype(BF16)
        send(SB.at[slot[2], :, lo:up], RF.at[2, :, lo:up], "rs", ("rf", h), zdev[2])
        t = KEEP[2, :, lo:up]
        came(("b1", h), RB1.at[:, lo:up])
        came(("b2", h), RB2.at[:, cut:up])
        t = t + RB1[:, lo:up].astype(F32)
        SB[slot[-2], :, lo:cut] = t[:, : cut - lo].astype(BF16)
        SB[slot[-2], :, cut:up] = (t[:, cut - lo :] + RB2[:, cut:up].astype(F32)).astype(BF16)
        send(SB.at[slot[-2], :, lo:up], RF.at[3, :, lo:up], "rs", ("rf", h), zdev[-2])

    rs_first(0)
    rs_first(1)
    rs_first(2)
    rs_near(0)
    came("m2", MZ)
    total = M2[...]
    for i in range(7):
        total = total + MZ[i]
    for i in range(7):
        U[:, 128 * i : 128 * (i + 1)] = total[i : i + 1, :]
    margin = q_target[...] - total[7:8, 0:48]
    weighting = jnp.where(margin > 0, expectile, 1.0 - expectile)
    VG[col] = jnp.zeros((8, 128), F32)
    VG[col, 0:1, 0:48] = -2.0 * value_scale * weighting * margin
    gather_direct(VG, "vg", "vg")
    came("gu1", GU.at[0, 0:2, 0])
    came("gu3", GU.at[0, 0:3, 0])
    for d in (-3, 3, 4):
        gu_y(d)
    rs_second(0)
    rs_near(1)
    rs_second(1)
    rs_near(2)
    rs_second(2)
    send(GU.at[yl, :, k], GU.at[yl, :, k], "gus", "gus1", sib)
    for h, (lo, _, up) in enumerate(PARTS):
        t = KEEP[0, :, lo:up]
        came(("rf", h), RF.at[:, :, lo:up])
        for i in range(4):
            t = t + RF[i, :, lo:up].astype(F32)
        OWNH[:, lo:up] = t
        YS[:, lo:up] = t.astype(BF16)
        send(YS.at[:, lo:up], YR.at[:, lo:up], "y", ("y", h), ylp)

    ready(l_no, l_gw, l_uw)
    GWT[...] = gw[...].T
    UWT[...] = uw[...].T

    came("gp1", GU.at[0, 0:2, 0])
    came("guy", GU.at[0, 0:5, 0])
    send(GU.at[1 - yl, :, k], GU.at[1 - yl, :, k], "gus", "gus2", sib)
    gather_y(NO, "no", "no")

    def h_at(d):
        return k * 8 + zd(d)

    def h_send(name, a, lo, up, to):
        send(HA.at[a, :, lo:up], HA.at[a, :, lo:up], "ha", name, to)

    for h, (lo, _, up) in enumerate(PARTS):
        came(("y", h), YR.at[:, lo:up])
        HA[h_at(0), :, lo:up] = (OWNH[:, lo:up] + YR[:, lo:up].astype(F32)).astype(BF16)
        for d in (2, -2):
            h_send(("h", d, h), h_at(0), lo, up, zdev[d])
    for lo, _, up in PARTS:
        for d in (1, -1):
            h_send("h1", h_at(0), lo, up, zdev[d])

    def h_forward(name, *ds):
        for d in ds:
            send(HA.at[h_at(d)], HA.at[h_at(d)], "has", name, sib)

    h_forward("s0", 0)

    came("vg", VG.at[0:15])

    def out_grad(j, carry):
        VC[j] = jnp.broadcast_to(VG[j].T[:48, 0:1], (48, 128))
        wide = jnp.concatenate([VC[j]] * 2, axis=1)
        OG[j] = (GO[j].astype(F32) + wide * vw).astype(BF16)
        return carry

    lax.fori_loop(0, 16, out_grad, 0, unroll=4)

    came("gus1", GU.at[yl, :, 1 - k])
    came("gus2", GU.at[1 - yl, :, 1 - k])

    def factors(j, carry):
        a = GU[j // 8, j % 8, 0].astype(F32)
        b = GU[j // 8, j % 8, 1].astype(F32)
        gate = jnp.concatenate([a[:24], b[:24]], axis=0)
        up = jnp.concatenate([a[24:], b[24:]], axis=0)
        s = jax.nn.sigmoid(gate)
        silu = gate * s
        SIL[j] = silu
        ACT[j] = (silu * up).astype(BF16)
        GF[j] = up * s * (1.0 + gate * (1.0 - s))
        return carry

    lax.fori_loop(0, 16, factors, 0)

    for h, (lo, cut, up) in enumerate(PARTS):
        came(("h", 2, h), HA.at[h_at(-2), :, lo:up])
        h_send("h3", h_at(-2), lo, up, zdev[1])
        h_send("h4", h_at(-2), lo, cut, zdev[2])
        came(("h", -2, h), HA.at[h_at(2), :, lo:up])
        h_send("h3", h_at(2), lo, up, zdev[-1])
        h_send("h4", h_at(2), cut, up, zdev[-2])
    h_forward("s2", -2, 2)
    came("h1", HA.at[0:2])
    h_forward("s1", -1, 1)

    gather_x(NO, "no", "no")
    def tokens(kk, *ds):
        js = [kk * 8 + zd(d) for d in ds]
        for j in js:
            h = HA[j].astype(F32) + jnp.concatenate([VC[j]] * 7, axis=1) * U[...]
            GB[j] = (h * GF[j]).astype(BF16)
            UB[j] = (h * SIL[j]).astype(BF16)
        g = jnp.concatenate([GB[j] for j in js], axis=0)
        u = jnp.concatenate([UB[j] for j in js], axis=0)
        part = dot(g, GWT[...]) + dot(u, UWT[...])
        for i, j in enumerate(js):
            mine = part[48 * i : 48 * (i + 1)]
            CS[j] = mine.astype(BF16)

            @pl.when(j == col)
            def _():
                OWN[...] = mine

            @pl.when(j != col)
            def _():
                remote(CS.at[j], RIN.at[col], "cs", "cs", (row, j)).start()

    def theirs(name, *ds):
        came(name, HA.at[pl.ds(0, len(ds))])
        return ds

    tokens(k, 0, -2, 2)
    tokens(1 - k, *theirs("s0", 0), *theirs("s2", -2, 2))
    tokens(k, -1, 1)
    tokens(1 - k, *theirs("s1", -1, 1))
    o_down[...] = dot_tn(ACT[...].reshape(768, 896), OG[...].reshape(768, 256)).astype(BF16)
    s_down = load(o_down, o_down_h)
    came("h3", HA.at[0:2])
    h_forward("s3", -3, 3)
    came("h4", HA.at[0])
    h_forward("s4", 4)
    tokens(k, -3, 3, 4)
    tokens(1 - k, *theirs("s3", -3, 3), *theirs("s4", 4))

    came("no", NO.at[0:12])
    NOT[...] = NO[...].reshape(768, 256).T
    o_gate[...] = dot(NOT[...], GB[...].reshape(768, 896)).astype(BF16)
    s_gate = load(o_gate, o_gate_h)
    o_up[...] = dot(NOT[...], UB[...].reshape(768, 896)).astype(BF16)
    s_up = load(o_up, o_up_h)

    left("go", GO.at[0:15])
    left("no", NO.at[0:15])
    left("vg", VG.at[0:15])
    left("guz", GU.at[0, 0:7, 0])
    left("gp", GU.at[0, 0:2, 0])
    left("guy", GU.at[0, 0:6, 0])
    left("gus", GU.at[0])
    left("gos", GOS)
    left("dw", DW.at[:, 256:])
    left("rs", SB.at[0:7])
    left("y", YS)
    left("ha", HA.at[0:7])
    left("has", HA.at[0:8])
    left("m0", M0)
    left("m1", M1)
    left("m2", MZ)

    remote(RIN.at[0:15], RIN.at[0:15], "cs", "cs", sib).wait()
    total = OWN[...]
    for i in range(1, 16):
        total = total + RIN[(col + i) % 16].astype(F32)
    o_normed[...] = total.astype(BF16)
    s_normed = load(o_normed, o_normed_h)
    for cp in (s_gate, s_up, s_down, s_normed):
        cp.wait()


def per_device(normed, gate_w, up_w, down_w, gate_pre, up_pre, block_out, value_w, q_target, grad_out):
    hbm = pl.BlockSpec(memory_space=pltpu.HBM)
    scratch = [
        pltpu.VMEM((16, 48, 256), BF16),
        pltpu.VMEM((8, 48, 256), BF16),
        pltpu.VMEM((16, 48, 256), BF16),
        pltpu.VMEM((2, 8, 2, 48, 896), BF16),
        pltpu.VMEM((256, 896), BF16),
        pltpu.VMEM((256, 896), BF16),
        pltpu.VMEM((896, 512), BF16),
        pltpu.VMEM((512, 896), BF16),
        pltpu.VMEM((896, 256), BF16),
        pltpu.VMEM((896, 256), BF16),
        pltpu.VMEM((256, 768), BF16),
        pltpu.VMEM((3, 48, 896), F32),
        pltpu.VMEM((8, 48, 896), BF16),
        pltpu.VMEM((48, 896), BF16),
        pltpu.VMEM((48, 896), BF16),
        pltpu.VMEM((48, 896), BF16),
        pltpu.VMEM((48, 896), BF16),
        pltpu.VMEM((4, 48, 896), BF16),
        pltpu.VMEM((48, 896), F32),
        pltpu.VMEM((48, 896), BF16),
        pltpu.VMEM((48, 896), BF16),
        pltpu.VMEM((16, 48, 896), BF16),
        pltpu.VMEM((16, 48, 896), F32),
        pltpu.VMEM((16, 48, 896), F32),
        pltpu.VMEM((16, 48, 896), BF16),
        pltpu.VMEM((16, 48, 896), BF16),
        pltpu.VMEM((16, 48, 896), BF16),
        pltpu.VMEM((16, 48, 256), BF16),
        pltpu.VMEM((16, 48, 256), BF16),
        pltpu.VMEM((16, 48, 256), BF16),
        pltpu.VMEM((48, 256), F32),
        pltpu.VMEM((48, 256), BF16),
        pltpu.VMEM((256, 896), BF16),
        pltpu.VMEM((256, 896), BF16),
        pltpu.VMEM((896, 256), BF16),
        pltpu.VMEM((24, 896), BF16),
        pltpu.VMEM((24, 896), BF16),
        pltpu.VMEM((48, 256), BF16),
        pltpu.VMEM((1, 256), F32),
        pltpu.VMEM((1, 48), F32),
        pltpu.VMEM((8, 128), F32),
        pltpu.VMEM((8, 128), F32),
        pltpu.VMEM((8, 128), F32),
        pltpu.VMEM((8, 128), F32),
        pltpu.VMEM((8, 128), F32),
        pltpu.VMEM((7, 8, 128), F32),
        pltpu.VMEM((16, 8, 128), F32),
        pltpu.VMEM((16, 48, 128), F32),
        pltpu.VMEM((1, 896), F32),
        pltpu.SemaphoreType.DMA((N_LOCAL,)),
        pltpu.SemaphoreType.DMA((N_SEND,)),
        pltpu.SemaphoreType.DMA((N_RECV,)),
    ]
    outs = pl.pallas_call(
        kernel,
        out_shape=(
            jax.ShapeDtypeStruct((48, 256), BF16),
            jax.ShapeDtypeStruct((256, 896), BF16),
            jax.ShapeDtypeStruct((256, 896), BF16),
            jax.ShapeDtypeStruct((896, 256), BF16),
        ),
        in_specs=[hbm] * 10,
        out_specs=(hbm, hbm, hbm, hbm),
        scratch_shapes=scratch,
        compiler_params=pltpu.CompilerParams(
            collective_id=0, has_side_effects=True, vmem_limit_bytes=VMEM_BYTES
        ),
    )(
        normed, gate_w, up_w, down_w, gate_pre, up_pre, block_out,
        value_w.reshape(1, 256), q_target.reshape(1, 48), grad_out,
    )
    return pl.pallas_call(
        hand_over,
        out_shape=tuple(jax.ShapeDtypeStruct(o.shape, o.dtype) for o in outs),
        in_specs=[hbm] * 4,
        out_specs=(hbm,) * 4,
        scratch_shapes=[pltpu.VMEM(o.shape, o.dtype) for o in outs]
        + [pltpu.SemaphoreType.DMA((4,)), pltpu.SemaphoreType.DMA((4,))],
        compiler_params=pltpu.CompilerParams(vmem_limit_bytes=VMEM_BYTES),
    )(*outs)


def hand_over(a, b, c, d, oa, ob, oc, od, va, vb, vc, vd, s_in, s_out):
    four = range(4)
    ins = [pltpu.make_async_copy((a, b, c, d)[i], (va, vb, vc, vd)[i], s_in.at[i]) for i in four]
    outs = [pltpu.make_async_copy((va, vb, vc, vd)[i], (oa, ob, oc, od)[i], s_out.at[i]) for i in four]
    for cp in ins:
        cp.start()
    for i in four:
        ins[i].wait()
        outs[i].start()
    for cp in outs:
        cp.wait()


def solution(mesh):
    return jax.shard_map(
        per_device,
        mesh=mesh,
        in_specs=(
            P("col", "row"),
            P("row", "col"),
            P("row", "col"),
            P("col", "row"),
            P("row", "col"),
            P("row", "col"),
            P("col", "row"),
            P("row"),
            P("col"),
            P("col", "row"),
        ),
        out_specs=(P("col", "row"), P("row", "col"), P("row", "col"), P("col", "row")),
        check_vma=False,
    )
```

```python
import jax
import jax.numpy as jnp
from jax import lax
from jax.experimental import pallas as pl
from jax.experimental.pallas import tpu as pltpu
from jax.sharding import PartitionSpec as P

expectile = 0.7
value_scale = 8.0

F32 = jnp.float32
BF16 = jnp.bfloat16
MESH = pl.DeviceIdType.MESH

PARTS = ((0, 128, 256), (256, 384, 512), (512, 640, 896))
CUT = 512
VMEM_BYTES = 60 * 2**20
N_SEND = 18
N_RECV = 58
N_LOCAL = 14

NT = (((1,), (1,)), ((), ()))
TN = (((0,), (0,)), ((), ()))


def dot_nt(a, b):
    return lax.dot_general(a, b, NT, preferred_element_type=F32)


def dot_tn(a, b):
    return lax.dot_general(a, b, TN, preferred_element_type=F32)


def dot(a, b):
    return jnp.dot(a, b, preferred_element_type=F32)


def kernel(
    normed_h, gate_w_h, up_w_h, down_w_h, gate_pre_h, up_pre_h, block_out_h, value_w_h, q_target_h, grad_out_h,
    o_normed_h, o_gate_h, o_up_h, o_down_h,
    GO, GOS, NO, GU, gw, uw, DW, DWT, GWT, UWT, NOT,
    KEEP, SB, RA1, RA2, RB1, RB2, RF, OWNH, YS, YR, HA,
    SIL, GF, ACT, GB, UB, OG,
    CS, RIN, OWN, o_normed, o_gate, o_up, o_down,
    gate_pre, up_pre, block_out, value_w, q_target, M0, MS, M1, MY, M2, MZ, VG, VC, U,
    local, ss, rs,
):
    row, col = lax.axis_index("row"), lax.axis_index("col")
    k, z, yl = row % 2, (row // 2) % 8, row // 16
    x, yh = col % 4, col // 4

    def dev(k_=k, z_=z, yl_=yl, x_=x, yh_=yh):
        return ((yl_ * 8 + z_) * 2 + k_, yh_ * 4 + x_)

    def zd(d):
        return (z + d + 8) % 8

    def xd(d):
        return (x + d + 4) % 4

    def yd(d):
        return (yh + d + 4) % 4

    sib = dev(k_=1 - k)
    ylp = dev(yl_=1 - yl)
    zdev = {d: dev(z_=zd(d)) for d in (1, -1, 2, -2, 3, -3, 4)}
    xdev = {d: dev(x_=xd(d)) for d in (1, 2, 3)}
    ydev = {d: dev(yh_=yd(d)) for d in (1, 2, 3)}

    ids = {"send": {}, "recv": {}}
    loads = []

    def sem(side, name):
        known = ids[side]
        if name not in known:
            known[name] = len(known)
            assert len(known) <= (N_SEND if side == "send" else N_RECV)
        return (ss if side == "send" else rs).at[known[name]]

    def remote(src, dst, group, name, to):
        return pltpu.make_async_remote_copy(
            src, dst, sem("send", group), sem("recv", name), device_id=to, device_id_type=MESH
        )

    def send(src, dst, group, name, to):
        remote(src, dst, group, name, to).start()

    def came(name, ref):
        remote(ref, ref, "none", name, sib).wait_recv()

    def left(group, ref):
        remote(ref, ref, group, "none", sib).wait_send()

    def load(src, dst):
        cp = pltpu.make_async_copy(src, dst, local.at[len(loads)])
        cp.start()
        loads.append(cp)
        return cp

    def ready(*cps):
        for cp in cps:
            cp.wait()

    barrier = pltpu.get_barrier_semaphore()
    partners = [sib, ylp, *zdev.values()] + [(row, (col + i) % 16) for i in range(1, 16)]
    for p in partners:
        pl.semaphore_signal(barrier, inc=1, device_id=p, device_id_type=MESH)

    l_go = load(grad_out_h, GO.at[col])
    l_gu = load(gate_pre_h, gate_pre), load(up_pre_h, up_pre)
    l_v = load(block_out_h, block_out), load(value_w_h, value_w), load(q_target_h, q_target)
    l_dw = load(down_w_h, DW.at[:, :256])
    l_no = load(normed_h, NO.at[col])
    l_gw = load(gate_w_h, gw)
    l_uw = load(up_w_h, uw)
    ready(l_go, *l_gu)
    GU[yl, z, k] = jnp.concatenate([gate_pre[...].astype(F32), up_pre[...].astype(F32)], axis=0).astype(BF16)
    pl.semaphore_wait(barrier, len(partners))

    def gather_direct(buf, group, name):
        for i in (10, 6, 14, 2, 9, 11, 5, 7, 13, 15, 1, 3, 8, 4, 12):
            send(buf.at[col], buf.at[col], group, name, (row, (col + i) % 16))

    def gather_y(buf, group, name):
        for d in (2, 1, 3):
            send(buf.at[col], buf.at[col], group, name + str(d), ydev[d])
        for d in (2, 1, 3):
            send(buf.at[col], buf.at[col], group, name, xdev[d])

    def gather_x(buf, group, name):
        for dy in (1, 3, 2):
            at = yd(-dy) * 4 + x
            came(name + str(dy), buf.at[at])
            for d in (2, 1, 3):
                send(buf.at[at], buf.at[at], group, name, xdev[d])

    gather_y(GO, "go", "go")

    def gu(d):
        return GU.at[yl, zd(d), k]

    def gu_y(d):
        send(gu(d), gu(d), "guy", "guy" if d else "gp0", ylp)

    for d, name in ((2, "gu+2"), (-2, "gu-2"), (1, "gu1"), (-1, "gu1")):
        send(gu(0), gu(0), "guz", name, zdev[d])
    gu_y(0)

    ready(l_dw, *l_v)
    vw = value_w[...]
    hi = vw.astype(BF16).astype(F32)
    mid = (vw - hi).astype(BF16).astype(F32)
    lo = vw - hi - mid
    terms = jnp.concatenate([hi, mid, lo, jnp.zeros((5, 256), F32)], axis=0).astype(BF16)
    send(DW.at[:, :256], DW.at[:, 256:], "dw", "dw", sib)
    u_part = jnp.sum(dot_nt(terms, DW[:, :256]), axis=0, keepdims=True)
    v_part = jnp.sum(dot_nt(terms, block_out[...]), axis=0, keepdims=True)
    M0[...] = jnp.zeros((8, 128), F32)
    for i in range(7):
        M0[i : i + 1, :] = u_part[:, 128 * i : 128 * (i + 1)]
    M0[7:8, 0:48] = v_part
    send(M0, MS, "m0", "m0", sib)

    gather_x(GO, "go", "go")

    came("m0", MS)
    M1[...] = M0[...] + MS[...]
    send(M1, MY, "m1", "m1", ylp)

    pair = GU.at[1 - yl, z, k]
    came("gp0", pair)
    for d in (1, -1):
        send(pair, pair, "gp", "gp1", zdev[d])
    came("gu+2", gu(-2))
    send(gu(-2), gu(-2), "guz", "gu3", zdev[1])
    send(gu(-2).at[:, :CUT], gu(-2).at[:, :CUT], "guz", "gu3", zdev[2])
    came("gu-2", gu(2))
    send(gu(2), gu(2), "guz", "gu3", zdev[-1])
    send(gu(2).at[:, CUT:], gu(2).at[:, CUT:], "guz", "gu3", zdev[-2])

    came("m1", MY)
    M2[...] = M1[...] + MY[...]
    for i, d in enumerate((4, 3, -3, 2, -2, 1, -1)):
        send(M2, MZ.at[i], "m2", "m2", zdev[d])

    gu_y(-2)
    gu_y(2)
    came("dw", DW.at[:, 256:])
    DWT[...] = DW[...].T
    came("go", GO.at[0:12])

    half = pl.ds((1 - k) * 8, 8)
    send(GO.at[half], GOS, "gos", "gos", sib)
    came("gos", GOS)
    slot = {d: i for i, d in enumerate((3, -3, 4, 2, -2, 1, -1))}

    def partial(ds, h):
        lo, _, up = PARTS[h]
        rows = [jnp.concatenate([GO[k * 8 + zd(d)], GOS[zd(d)]], axis=1) for d in ds]
        p = dot(jnp.concatenate(rows, axis=0), DWT[:, lo:up])
        return [p[48 * i : 48 * (i + 1)] for i in range(len(ds))]

    def rs_first(h):
        lo, cut, up = PARTS[h]
        for d, p in zip((4, 3, -3, 2), partial((4, 3, -3, 2), h)):
            if d == 2:
                KEEP[1, :, lo:up] = p
                continue
            SB[slot[d], :, lo:up] = p.astype(BF16)
            src = SB.at[slot[d]]
            if d == 3:
                send(src.at[:, lo:up], RA1.at[:, lo:up], "rs", ("a1", h), zdev[1])
            elif d == -3:
                send(src.at[:, lo:up], RB1.at[:, lo:up], "rs", ("b1", h), zdev[-1])
            else:
                send(src.at[:, lo:cut], RA2.at[:, lo:cut], "rs", ("a2", h), zdev[2])
                send(src.at[:, cut:up], RB2.at[:, cut:up], "rs", ("b2", h), zdev[-2])

    def rs_near(h):
        lo, cut, up = PARTS[h]
        p = partial((1, -1, -2, 0), h)
        for i, d in enumerate((1, -1)):
            SB[slot[d], :, lo:up] = p[i].astype(BF16)
            send(SB.at[slot[d], :, lo:up], RF.at[i, :, lo:up], "rs", ("rf", h), zdev[d])
        KEEP[2, :, lo:up] = p[2]
        KEEP[0, :, lo:up] = p[3]

    def rs_second(h):
        lo, cut, up = PARTS[h]
        t = KEEP[1, :, lo:up]
        came(("a1", h), RA1.at[:, lo:up])
        came(("a2", h), RA2.at[:, lo:cut])
        t = t + RA1[:, lo:up].astype(F32)
        SB[slot[2], :, lo:cut] = (t[:, : cut - lo] + RA2[:, lo:cut].astype(F32)).astype(BF16)
        SB[slot[2], :, cut:up] = t[:, cut - lo :].astype(BF16)
        send(SB.at[slot[2], :, lo:up], RF.at[2, :, lo:up], "rs", ("rf", h), zdev[2])
        t = KEEP[2, :, lo:up]
        came(("b1", h), RB1.at[:, lo:up])
        came(("b2", h), RB2.at[:, cut:up])
        t = t + RB1[:, lo:up].astype(F32)
        SB[slot[-2], :, lo:cut] = t[:, : cut - lo].astype(BF16)
        SB[slot[-2], :, cut:up] = (t[:, cut - lo :] + RB2[:, cut:up].astype(F32)).astype(BF16)
        send(SB.at[slot[-2], :, lo:up], RF.at[3, :, lo:up], "rs", ("rf", h), zdev[-2])

    rs_first(0)
    rs_first(1)
    rs_first(2)
    rs_near(0)
    came("m2", MZ)
    total = M2[...]
    for i in range(7):
        total = total + MZ[i]
    for i in range(7):
        U[:, 128 * i : 128 * (i + 1)] = total[i : i + 1, :]
    margin = q_target[...] - total[7:8, 0:48]
    weighting = jnp.where(margin > 0, expectile, 1.0 - expectile)
    VG[col] = jnp.zeros((8, 128), F32)
    VG[col, 0:1, 0:48] = -2.0 * value_scale * weighting * margin
    gather_direct(VG, "vg", "vg")
    came("gu1", GU.at[0, 0:2, 0])
    came("gu3", GU.at[0, 0:3, 0])
    for d in (-3, 3, 4):
        gu_y(d)
    rs_second(0)
    rs_near(1)
    rs_second(1)
    rs_near(2)
    rs_second(2)
    send(GU.at[yl, :, k], GU.at[yl, :, k], "gus", "gus1", sib)
    for h, (lo, _, up) in enumerate(PARTS):
        t = KEEP[0, :, lo:up]
        came(("rf", h), RF.at[:, :, lo:up])
        for i in range(4):
            t = t + RF[i, :, lo:up].astype(F32)
        OWNH[:, lo:up] = t
        YS[:, lo:up] = t.astype(BF16)
        send(YS.at[:, lo:up], YR.at[:, lo:up], "y", ("y", h), ylp)

    ready(l_no, l_gw, l_uw)
    GWT[...] = gw[...].T
    UWT[...] = uw[...].T

    came("gp1", GU.at[0, 0:2, 0])
    came("guy", GU.at[0, 0:5, 0])
    send(GU.at[1 - yl, :, k], GU.at[1 - yl, :, k], "gus", "gus2", sib)
    gather_y(NO, "no", "no")

    def h_at(d):
        return k * 8 + zd(d)

    def h_send(name, a, lo, up, to):
        send(HA.at[a, :, lo:up], HA.at[a, :, lo:up], "ha", name, to)

    for h, (lo, _, up) in enumerate(PARTS):
        came(("y", h), YR.at[:, lo:up])
        HA[h_at(0), :, lo:up] = (OWNH[:, lo:up] + YR[:, lo:up].astype(F32)).astype(BF16)
        for d in (2, -2):
            h_send(("h", d, h), h_at(0), lo, up, zdev[d])
    for lo, _, up in PARTS:
        for d in (1, -1):
            h_send("h1", h_at(0), lo, up, zdev[d])

    def h_forward(name, *ds):
        for d in ds:
            send(HA.at[h_at(d)], HA.at[h_at(d)], "has", name, sib)

    h_forward("s0", 0)

    came("vg", VG.at[0:15])

    def out_grad(j, carry):
        VC[j] = jnp.broadcast_to(VG[j].T[:48, 0:1], (48, 128))
        wide = jnp.concatenate([VC[j]] * 2, axis=1)
        OG[j] = (GO[j].astype(F32) + wide * vw).astype(BF16)
        return carry

    lax.fori_loop(0, 16, out_grad, 0, unroll=4)

    came("gus1", GU.at[yl, :, 1 - k])
    came("gus2", GU.at[1 - yl, :, 1 - k])

    def factors(j, carry):
        a = GU[j // 8, j % 8, 0].astype(F32)
        b = GU[j // 8, j % 8, 1].astype(F32)
        gate = jnp.concatenate([a[:24], b[:24]], axis=0)
        up = jnp.concatenate([a[24:], b[24:]], axis=0)
        s = jax.nn.sigmoid(gate)
        silu = gate * s
        SIL[j] = silu
        ACT[j] = (silu * up).astype(BF16)
        GF[j] = up * s * (1.0 + gate * (1.0 - s))
        return carry

    lax.fori_loop(0, 16, factors, 0)

    for h, (lo, cut, up) in enumerate(PARTS):
        came(("h", 2, h), HA.at[h_at(-2), :, lo:up])
        h_send("h4", h_at(-2), lo, cut, zdev[2])
        h_send("h3", h_at(-2), lo, up, zdev[1])
        came(("h", -2, h), HA.at[h_at(2), :, lo:up])
        h_send("h4", h_at(2), cut, up, zdev[-2])
        h_send("h3", h_at(2), lo, up, zdev[-1])
    h_forward("s2", -2, 2)
    came("h1", HA.at[0:2])
    h_forward("s1", -1, 1)

    gather_x(NO, "no", "no")
    def tokens(kk, *ds):
        js = [kk * 8 + zd(d) for d in ds]
        for j in js:
            h = HA[j].astype(F32) + jnp.concatenate([VC[j]] * 7, axis=1) * U[...]
            GB[j] = (h * GF[j]).astype(BF16)
            UB[j] = (h * SIL[j]).astype(BF16)
        g = jnp.concatenate([GB[j] for j in js], axis=0)
        u = jnp.concatenate([UB[j] for j in js], axis=0)
        part = dot(g, GWT[...]) + dot(u, UWT[...])
        for i, j in enumerate(js):
            mine = part[48 * i : 48 * (i + 1)]
            CS[j] = mine.astype(BF16)

            @pl.when(j == col)
            def _():
                OWN[...] = mine

            @pl.when(j != col)
            def _():
                remote(CS.at[j], RIN.at[col], "cs", "cs", (row, j)).start()

    def theirs(name, *ds):
        came(name, HA.at[pl.ds(0, len(ds))])
        return ds

    tokens(k, 0, -2, 2)
    tokens(1 - k, *theirs("s0", 0), *theirs("s2", -2, 2))
    tokens(k, -1, 1)
    tokens(1 - k, *theirs("s1", -1, 1))
    o_down[...] = dot_tn(ACT[...].reshape(768, 896), OG[...].reshape(768, 256)).astype(BF16)
    s_down = load(o_down, o_down_h)
    came("h3", HA.at[0:2])
    h_forward("s3", -3, 3)
    came("h4", HA.at[0])
    h_forward("s4", 4)
    tokens(k, -3, 3, 4)
    tokens(1 - k, *theirs("s3", -3, 3), *theirs("s4", 4))

    came("no", NO.at[0:12])
    NOT[...] = NO[...].reshape(768, 256).T
    o_gate[...] = dot(NOT[...], GB[...].reshape(768, 896)).astype(BF16)
    s_gate = load(o_gate, o_gate_h)
    o_up[...] = dot(NOT[...], UB[...].reshape(768, 896)).astype(BF16)
    s_up = load(o_up, o_up_h)

    left("go", GO.at[0:15])
    left("no", NO.at[0:15])
    left("vg", VG.at[0:15])
    left("guz", GU.at[0, 0:7, 0])
    left("gp", GU.at[0, 0:2, 0])
    left("guy", GU.at[0, 0:6, 0])
    left("gus", GU.at[0])
    left("gos", GOS)
    left("dw", DW.at[:, 256:])
    left("rs", SB.at[0:7])
    left("y", YS)
    left("ha", HA.at[0:7])
    left("has", HA.at[0:8])
    left("m0", M0)
    left("m1", M1)
    left("m2", MZ)

    remote(RIN.at[0:15], RIN.at[0:15], "cs", "cs", sib).wait()
    total = OWN[...]
    for i in range(1, 16):
        total = total + RIN[(col + i) % 16].astype(F32)
    o_normed[...] = total.astype(BF16)
    s_normed = load(o_normed, o_normed_h)
    for cp in (s_gate, s_up, s_down, s_normed):
        cp.wait()


def per_device(normed, gate_w, up_w, down_w, gate_pre, up_pre, block_out, value_w, q_target, grad_out):
    hbm = pl.BlockSpec(memory_space=pltpu.HBM)
    scratch = [
        pltpu.VMEM((16, 48, 256), BF16),
        pltpu.VMEM((8, 48, 256), BF16),
        pltpu.VMEM((16, 48, 256), BF16),
        pltpu.VMEM((2, 8, 2, 48, 896), BF16),
        pltpu.VMEM((256, 896), BF16),
        pltpu.VMEM((256, 896), BF16),
        pltpu.VMEM((896, 512), BF16),
        pltpu.VMEM((512, 896), BF16),
        pltpu.VMEM((896, 256), BF16),
        pltpu.VMEM((896, 256), BF16),
        pltpu.VMEM((256, 768), BF16),
        pltpu.VMEM((3, 48, 896), F32),
        pltpu.VMEM((8, 48, 896), BF16),
        pltpu.VMEM((48, 896), BF16),
        pltpu.VMEM((48, 896), BF16),
        pltpu.VMEM((48, 896), BF16),
        pltpu.VMEM((48, 896), BF16),
        pltpu.VMEM((4, 48, 896), BF16),
        pltpu.VMEM((48, 896), F32),
        pltpu.VMEM((48, 896), BF16),
        pltpu.VMEM((48, 896), BF16),
        pltpu.VMEM((16, 48, 896), BF16),
        pltpu.VMEM((16, 48, 896), F32),
        pltpu.VMEM((16, 48, 896), F32),
        pltpu.VMEM((16, 48, 896), BF16),
        pltpu.VMEM((16, 48, 896), BF16),
        pltpu.VMEM((16, 48, 896), BF16),
        pltpu.VMEM((16, 48, 256), BF16),
        pltpu.VMEM((16, 48, 256), BF16),
        pltpu.VMEM((16, 48, 256), BF16),
        pltpu.VMEM((48, 256), F32),
        pltpu.VMEM((48, 256), BF16),
        pltpu.VMEM((256, 896), BF16),
        pltpu.VMEM((256, 896), BF16),
        pltpu.VMEM((896, 256), BF16),
        pltpu.VMEM((24, 896), BF16),
        pltpu.VMEM((24, 896), BF16),
        pltpu.VMEM((48, 256), BF16),
        pltpu.VMEM((1, 256), F32),
        pltpu.VMEM((1, 48), F32),
        pltpu.VMEM((8, 128), F32),
        pltpu.VMEM((8, 128), F32),
        pltpu.VMEM((8, 128), F32),
        pltpu.VMEM((8, 128), F32),
        pltpu.VMEM((8, 128), F32),
        pltpu.VMEM((7, 8, 128), F32),
        pltpu.VMEM((16, 8, 128), F32),
        pltpu.VMEM((16, 48, 128), F32),
        pltpu.VMEM((1, 896), F32),
        pltpu.SemaphoreType.DMA((N_LOCAL,)),
        pltpu.SemaphoreType.DMA((N_SEND,)),
        pltpu.SemaphoreType.DMA((N_RECV,)),
    ]
    outs = pl.pallas_call(
        kernel,
        out_shape=(
            jax.ShapeDtypeStruct((48, 256), BF16),
            jax.ShapeDtypeStruct((256, 896), BF16),
            jax.ShapeDtypeStruct((256, 896), BF16),
            jax.ShapeDtypeStruct((896, 256), BF16),
        ),
        in_specs=[hbm] * 10,
        out_specs=(hbm, hbm, hbm, hbm),
        scratch_shapes=scratch,
        compiler_params=pltpu.CompilerParams(
            collective_id=0, has_side_effects=True, vmem_limit_bytes=VMEM_BYTES
        ),
    )(
        normed, gate_w, up_w, down_w, gate_pre, up_pre, block_out,
        value_w.reshape(1, 256), q_target.reshape(1, 48), grad_out,
    )
    return pl.pallas_call(
        hand_over,
        out_shape=tuple(jax.ShapeDtypeStruct(o.shape, o.dtype) for o in outs),
        in_specs=[hbm] * 4,
        out_specs=(hbm,) * 4,
        scratch_shapes=[pltpu.VMEM(o.shape, o.dtype) for o in outs]
        + [pltpu.SemaphoreType.DMA((4,)), pltpu.SemaphoreType.DMA((4,))],
        compiler_params=pltpu.CompilerParams(vmem_limit_bytes=VMEM_BYTES),
    )(*outs)


def hand_over(a, b, c, d, oa, ob, oc, od, va, vb, vc, vd, s_in, s_out):
    four = range(4)
    ins = [pltpu.make_async_copy((a, b, c, d)[i], (va, vb, vc, vd)[i], s_in.at[i]) for i in four]
    outs = [pltpu.make_async_copy((va, vb, vc, vd)[i], (oa, ob, oc, od)[i], s_out.at[i]) for i in four]
    for cp in ins:
        cp.start()
    for i in four:
        ins[i].wait()
        outs[i].start()
    for cp in outs:
        cp.wait()


def solution(mesh):
    return jax.shard_map(
        per_device,
        mesh=mesh,
        in_specs=(
            P("col", "row"),
            P("row", "col"),
            P("row", "col"),
            P("col", "row"),
            P("row", "col"),
            P("row", "col"),
            P("col", "row"),
            P("row"),
            P("col"),
            P("col", "row"),
        ),
        out_specs=(P("col", "row"), P("row", "col"), P("row", "col"), P("col", "row")),
        check_vma=False,
    )
```
